512 devices in a mesh: rep: 4 (over y), samp: 4 (over z_hi), tp: 32 (over z_lo, x, core).
Axes of the slice: x: 4, y: 4, z: 16 (z_hi: 4, z_lo: 4; z = z_hi * 4 + z_lo), core: 2. Of those that a mesh axis runs over, the one named last changes fastest.
Arguments:
- prompt_tokens: bfloat16 [256, 4, 8192], P(None, 'rep', 'samp'), may hold values from -6 to 6
- step_tokens: bfloat16 [4, 16, 4, 8192], P(None, None, 'rep', 'samp'), may hold values from -6 to 6
- lengths: int32 [16, 4], P('samp', 'rep'), may hold values from 1 to 4, as said below
- input_weight: bfloat16 [2, 8192, 8192], P(None, 'samp', 'tp'), may hold values from -0.0625 to 0.0625
- group_weight: bfloat16 [8192, 2048], P('samp', 'tp'), may hold values from -0.0625 to 0.0625
- step_weight: bfloat16 [8192, 128], P('samp', 'tp'), may hold values from -0.0625 to 0.0625
- conv_weight: float32 [4, 8192], P(None, 'tp'), may hold values from -3 to 3
- group_conv: float32 [4, 2048], P(None, 'tp'), may hold values from -3 to 3
- conv_bias: float32 [8192], P('tp'), may hold values from -3 to 3
- group_bias: float32 [2048], P('tp'), may hold values from -3 to 3
- step_bias: float32 [128], P('tp'), may hold values from -3 to -1
- decay_log: float32 [128], P('tp'), may hold values from -4.6 to -1.6
- skip_gain: float32 [128], P('tp'), may hold values from 0.5 to 1.5
- norm_gain: float32 [8192], P('tp'), may hold values from 0.5 to 1.5
- output_weight: bfloat16 [8192, 8192], P('tp', 'samp'), may hold values from -0.125 to 0.125
Outputs:
- prefill_out: bfloat16 [256, 4, 8192], P('samp', 'rep', 'tp')
- decode_out: bfloat16 [4, 16, 4, 8192], P(None, 'samp', 'rep', 'tp')
The draws below stay inside these ranges and needn't reach their ends.
Inputs may be any that keep to these rules, and one draw needn't show every extreme that they name: `lengths`: every prompt has a sample that decodes all 4 steps.
All inputs are finite; a program needn't handle non-finite values.
Results may differ from the reference program's by a relative error of at most 0.035.
Values may be sent and summed in bfloat16 or wider, within the bound.
A program may use at most 64 MiB of HBM per device.

```python
import jax
import jax.numpy as jnp
from jax import lax

D = 8192
HEADS = 128
HEAD_DIM = 64
STATE = 128
GROUPS = 8
CONV = 4
L = 256
SAMPLES = 16
STEPS = 4
PROMPTS = 4
INNER = 8192
BC = 2048
DQ = 2048
INNER_DEV = 256


def draw_lengths(key, part):
    key = jax.random.fold_in(key, 7)
    first_key, second_key = jax.random.split(key)
    drawn_lengths = jax.random.randint(first_key, (SAMPLES, PROMPTS), 1, STEPS + 1)
    chosen = jax.random.randint(second_key, (1, PROMPTS), 0, SAMPLES)
    sample_rows = jnp.arange(SAMPLES)[:, None]
    return jnp.where(sample_rows == chosen, STEPS, drawn_lengths).astype(jnp.int32)


def strengthened(values, stream_key, source, target, parts, factor):
    owner, partner = [(jnp.arange(values.shape[dim]) // (values.shape[dim] // parts)).reshape([-1 if axis == dim else 1 for axis in range(values.ndim)]) for dim in (source, target)]
    chosen = jax.random.permutation(stream_key, parts)[partner]
    strong = (owner == chosen) | (owner == (partner + parts // 2) % parts)
    return jnp.where(strong, factor * values, values)


def levels(key, extent, cuts, least, high):
    def one(dim, shards_of):
        heights = jax.random.uniform(jax.random.fold_in(jax.random.fold_in(key, 6), dim), (shards_of,), jnp.float32, least / len(cuts), high / len(cuts))
        return jnp.repeat(jnp.exp(heights), extent[dim] // shards_of).reshape((-1,) + (1,) * (len(extent) - dim - 1))

    gain = one(*cuts[0])
    for cut in cuts[1:]:
        gain = gain * one(*cut)
    return gain


def gaussian(key, dims, deviation, reach, cuts=(), kind=jnp.bfloat16):
    gain = levels(key, dims, cuts, -0.22, 0.18) if cuts else 1.0
    values = jax.random.normal(key, dims, jnp.float32) * deviation * gain
    return jnp.minimum(jnp.maximum(values, -reach), reach).astype(kind)


def heavy_noise(stream_key, shape, spread, reach, cuts, heavy, kind=jnp.bfloat16):
    values = spread * jax.random.normal(stream_key, shape, jnp.float32)
    if cuts:
        values = values * levels(stream_key, shape, cuts, -0.22, 0.18)
    return jnp.clip(strengthened(values, jax.random.fold_in(stream_key, 3), *heavy), -reach, reach).astype(kind)


def setup_inputs(seed: int = 0) -> dict:
    splits = jax.random.split(jax.random.key(seed), 16)
    prompt_tokens = gaussian(splits[0], (L, PROMPTS, D), 1.0, 6.0, ((1, 4), (2, 4)))
    step_tokens = gaussian(splits[1], (STEPS, SAMPLES, PROMPTS, D), 1.0, 6.0, ((2, 4), (3, 4)))
    lengths = draw_lengths(jax.random.fold_in(splits[15], 71), 0)
    input_weight = gaussian(splits[3], (2, D, INNER), D ** -0.5, 0.0625, ((1, 4), (2, 32)))
    group_weight = gaussian(splits[4], (D, BC), D ** -0.5, 0.0625, ((0, 4), (1, 32)))
    step_weight = gaussian(splits[5], (D, HEADS), D ** -0.5, 0.0625, ((0, 4), (1, 32)))
    conv_weight = gaussian(splits[6], (CONV, INNER), CONV ** -0.5, 3.0, ((1, 32),), jnp.float32)
    group_conv = gaussian(splits[7], (CONV, BC), CONV ** -0.5, 3.0, ((1, 32),), jnp.float32)
    conv_bias = gaussian(splits[8], (INNER,), 0.5, 3.0, ((0, 32),), jnp.float32)
    group_bias = gaussian(splits[9], (BC,), 0.5, 3.0, ((0, 32),), jnp.float32)
    step_bias = jnp.clip(-3.0 + 2.0 * jax.random.uniform(splits[10], (HEADS,), jnp.float32) ** levels(splits[10], (HEADS,), ((0, 32),), -0.2, 0.2), -3.0, -1.0)
    decay_log = jnp.clip(-4.6 + 3 * jax.random.uniform(splits[11], (HEADS,), jnp.float32) ** levels(splits[11], (HEADS,), ((0, 32),), -0.2, 0.2), -4.6, -1.6)
    skip_gain = jnp.clip(0.5 + 1.0 * jax.random.uniform(splits[12], (HEADS,), jnp.float32) ** levels(splits[12], (HEADS,), ((0, 32),), -0.2, 0.2), 0.5, 1.5)
    norm_gain = jnp.clip(1.0 + 0.1 * jax.random.normal(splits[13], (INNER,), jnp.float32), 0.5, 1.5)
    output_weight = heavy_noise(splits[14], (INNER, D), INNER ** -0.5, 0.125, ((0, 32), (1, 4)), (0, 1, 32, 2.75))
    return dict(prompt_tokens=prompt_tokens, step_tokens=step_tokens, lengths=lengths, input_weight=input_weight, group_weight=group_weight, step_weight=step_weight, conv_weight=conv_weight, group_conv=group_conv, conv_bias=conv_bias, group_bias=group_bias, step_bias=step_bias, decay_log=decay_log, skip_gain=skip_gain, norm_gain=norm_gain, output_weight=output_weight)


def rounded(value):
    return lax.optimization_barrier(value.astype(jnp.bfloat16)).astype(jnp.float32)

def project_in(tokens, input_weight, group_weight, step_weight):
    weights = jnp.concatenate([input_weight[0], input_weight[1], group_weight, step_weight], axis=1)
    running = jnp.zeros(tokens.shape[:-1] + (weights.shape[1],), jnp.float32)
    for slice_index in range(D // DQ):
        low_row = slice_index * DQ
        piece = jnp.dot(tokens[..., low_row:low_row + DQ], weights[low_row:low_row + DQ], preferred_element_type=jnp.float32)
        running = running + rounded(piece)
    return running.astype(jnp.bfloat16)

def convolve(window, tap_weight, tap_bias):
    length = window.shape[0] - CONV + 1
    running = jnp.zeros(window[:length].shape, jnp.float32) + tap_bias
    for tap_index in range(CONV):
        running = running + tap_weight[tap_index] * window[tap_index:tap_index + length].astype(jnp.float32)
    return jax.nn.silu(running).astype(jnp.bfloat16)

def split_heads(mixed):
    leading = mixed.shape[:-1]
    head_values = mixed[..., :INNER].astype(jnp.float32).reshape(leading + (HEADS, HEAD_DIM))
    grouped = mixed[..., INNER:].astype(jnp.float32).reshape(leading + (2, STATE, GROUPS))
    per_group = HEADS // GROUPS
    input_map = jnp.repeat(jnp.swapaxes(grouped[..., 0, :, :], -1, -2), per_group, axis=-2)
    output_map = jnp.repeat(jnp.swapaxes(grouped[..., 1, :, :], -1, -2), per_group, axis=-2)
    return (head_values, input_map, output_map)

def advance(state, head_values, input_map, output_map, step_size, decay, skip_gain):
    fresh = decay[..., None, None] * state + (step_size[..., None] * head_values)[..., None] * input_map[..., None, :]
    reading = lax.optimization_barrier(jnp.sum(fresh * output_map[..., None, :], axis=-1)) + skip_gain[:, None] * head_values
    return (fresh, reading)

def finish(reading, gate_rows, norm_gain, output_weight):
    leading = reading.shape[:-2]
    gated = reading.reshape(leading + (INNER,)) * jax.nn.silu(gate_rows.astype(jnp.float32))
    grouped = gated.reshape(leading + (GROUPS, INNER // GROUPS))
    scale = lax.rsqrt(lax.optimization_barrier(jnp.mean(grouped * grouped, axis=-1, keepdims=True)) + 1e-05)
    normed = ((grouped * scale).reshape(leading + (INNER,)) * norm_gain).astype(jnp.bfloat16)
    running = jnp.zeros(leading + (D,), jnp.float32)
    for shard_index in range(INNER // INNER_DEV):
        low_row = shard_index * INNER_DEV
        piece = jnp.dot(normed[..., low_row:low_row + INNER_DEV], output_weight[low_row:low_row + INNER_DEV], preferred_element_type=jnp.float32)
        running = running + rounded(piece)
    return running.astype(jnp.bfloat16)

def reference(prompt_tokens, step_tokens, lengths, input_weight, group_weight, step_weight, conv_weight, group_conv, conv_bias, group_bias, step_bias, decay_log, skip_gain, norm_gain, output_weight):
    tap_weight = jnp.concatenate([conv_weight, group_conv], axis=1)
    tap_bias = jnp.concatenate([conv_bias, group_bias])
    rate = jnp.exp(decay_log)
    projected = project_in(prompt_tokens, input_weight, group_weight, step_weight)
    mixed_pre = projected[..., INNER:2 * INNER + BC]
    padded = jnp.concatenate([jnp.zeros((CONV - 1,) + mixed_pre.shape[1:], jnp.bfloat16), mixed_pre], axis=0)
    head_values, input_map, output_map = split_heads(convolve(padded, tap_weight, tap_bias))
    step_size = jax.nn.softplus(projected[..., 2 * INNER + BC:].astype(jnp.float32) + step_bias)
    decay = jnp.exp(-step_size * rate)

    def token_step(state, pieces):
        values_now, inputs_now, readout_now, size_now, decay_now = pieces
        return advance(state, values_now, inputs_now, readout_now, size_now, decay_now, skip_gain)
    start_state = jnp.zeros((PROMPTS, HEADS, HEAD_DIM, STATE), jnp.float32)
    final_state, readings = lax.scan(token_step, start_state, (head_values, input_map, output_map, step_size, decay))
    prefill_out = finish(readings, projected[..., :INNER], norm_gain, output_weight)
    state = jnp.broadcast_to(final_state[None], (SAMPLES,) + final_state.shape)
    window = jnp.broadcast_to(mixed_pre[-(CONV - 1):][:, None], (CONV - 1, SAMPLES) + mixed_pre.shape[1:])
    results = []
    for step_index in range(STEPS):
        fresh = project_in(step_tokens[step_index], input_weight, group_weight, step_weight)
        full_window = jnp.concatenate([window, fresh[..., INNER:2 * INNER + BC][None]], axis=0)
        values_now, inputs_now, readout_now = split_heads(convolve(full_window, tap_weight, tap_bias)[0])
        size_now = jax.nn.softplus(fresh[..., 2 * INNER + BC:].astype(jnp.float32) + step_bias)
        advanced, reading = advance(state, values_now, inputs_now, readout_now, size_now, jnp.exp(-size_now * rate), skip_gain)
        active = step_index < lengths
        state = jnp.where(active[..., None, None, None], advanced, state)
        window = jnp.where(active[None, ..., None], full_window[1:], window)
        produced = finish(reading, fresh[..., :INNER], norm_gain, output_weight)
        results.append(jnp.where(active[..., None], produced, jnp.zeros_like(produced)))
    return (prefill_out, jnp.stack(results))
```

```python
import jax
import jax.numpy as jnp
from jax import lax
from jax.experimental import pallas as pl
from jax.experimental.pallas import tpu as pltpu
from jax.sharding import PartitionSpec as P

PROMPT = 256
FRESH = 64
ROWS = 320
PADDED = 384
WIDTH = 2048
CHANNELS = 256
BLOCK = 80
MSG = 336
MESH = pl.DeviceIdType.MESH
F32 = jnp.float32
BF16 = jnp.bfloat16
NT = (((1,), (1,)), ((), ()))


def mm(a, b):
    return jnp.dot(a, b, preferred_element_type=F32)


def mm_nt(a, b):
    return lax.dot_general(a, b, NT, preferred_element_type=F32)


def iota(shape, axis):
    return lax.broadcasted_iota(jnp.int32, shape, axis)


def silu(v):
    return v / (1.0 + jnp.exp(-v))


def kernel(
    prompt_ref, fresh_ref, in_ref, group_ref, out_ref,
    step_ref, taps_ref, bias_ref, group_taps_ref, group_bias_ref,
    step_bias_ref, decay_ref, skip_ref, gain_ref,
    prefill_ref, decode_ref,
    tokens, w_in, w_group, w_out, load_sem,
    packed_taps, a_src, a_dst, b_src, b_dst, maps, rs_src, rs_dst,
    mixed, gat, wide, sq_src, sq_dst, normed,
    d1_src, d1_dst, own, d2_src, d2_dst, d3_src, d3_dst,
    a_send, a_recv, b_send, b_recv, c_send, c_recv, rs_send, rs_recv,
    g_send, g_recv, q_send, q_recv, d1_send, d1_recv, d2_send, d2_recv, d3_send, d3_recv,
):
    rep = lax.axis_index("rep")
    samp = lax.axis_index("samp")
    tp = lax.axis_index("tp")
    low = tp // 8
    place = tp % 8
    across = place // 2
    core = place % 2
    group = tp // 4
    quarter = tp % 4

    def device(samp_index, tp_index):
        return (rep, samp_index, tp_index)

    barrier = pltpu.get_barrier_semaphore()

    def greet(samp_index, tp_index):
        pl.semaphore_signal(barrier, inc=1, device_id=device(samp_index, tp_index), device_id_type=MESH)

    for d in range(1, 4):
        greet((samp + d) % 4, tp)
        greet(samp, group * 4 + (quarter + d) % 4)
        greet(samp, low * 8 + ((across + d) % 4) * 2 + core)
    for i in range(8):
        @pl.when(quarter * 8 + i != tp)
        def _():
            greet(samp, quarter * 8 + i)
    for i in range(4):
        @pl.when(jnp.logical_or(low != samp, i != low))
        def _():
            greet(low, i * 8 + place)

    loads = [
        pltpu.make_async_copy(group_ref, w_group, load_sem.at[0]),
        pltpu.make_async_copy(prompt_ref, tokens.at[pl.ds(0, PROMPT)], load_sem.at[1]),
        pltpu.make_async_copy(fresh_ref, tokens.at[pl.ds(PROMPT, FRESH)], load_sem.at[2]),
        pltpu.make_async_copy(in_ref, w_in, load_sem.at[3]),
        pltpu.make_async_copy(out_ref, w_out, load_sem.at[4]),
    ]
    for load in loads:
        load.start()
    tokens[pl.ds(ROWS, PADDED - ROWS), :] = jnp.zeros((PADDED - ROWS, WIDTH), BF16)

    packed_taps[...] = jnp.zeros(packed_taps.shape, F32)
    for at, value in ((64, group_taps_ref[...]), (68, group_bias_ref[...])):
        high = value.astype(BF16).astype(F32)
        packed_taps[pl.ds(at, value.shape[0]), :] = high
        packed_taps[pl.ds(at + 8, value.shape[0]), :] = value - high

    row = iota((64, 64), 0)
    col = iota((64, 64), 1)
    regroup = (col == (row % 8) * 8 + row // 8).astype(F32).astype(BF16)
    requarter = (col == ((row % 16) // 4) * 16 + (row // 16) * 4 + row % 4).astype(F32).astype(BF16)

    for load in loads[:3]:
        load.wait()
    maps_partial = mm_nt(w_group[...], tokens[...]).astype(BF16)
    regrouped = mm(regroup, maps_partial)
    tail = regrouped[:, PROMPT:] + mm_nt(regroup, packed_taps[...].astype(BF16))
    a_src[:, :, pl.ds(0, PROMPT)] = regrouped[:, :PROMPT].reshape(8, 8, PROMPT).astype(BF16)
    a_src[:, :, pl.ds(PROMPT, 128)] = tail.reshape(8, 8, 128).astype(BF16)

    pl.semaphore_wait(
        barrier, 19 + jnp.where(quarter != low, 1, 0) + jnp.where(samp != low, 1, 0)
    )

    def a_copy(g):
        return pltpu.make_async_remote_copy(
            src_ref=a_src.at[g], dst_ref=a_dst.at[place],
            send_sem=a_send.at[g], recv_sem=a_recv.at[place],
            device_id=device(samp, g * 4 + low), device_id_type=MESH,
        )

    for g in range(8):
        @pl.when(g * 4 + low != tp)
        def _():
            a_copy(g).start()

        @pl.when(g * 4 + low == tp)
        def _():
            a_dst[pl.ds(place, 1)] = a_src[pl.ds(g, 1)]

    sizes = mm_nt(step_ref[...], tokens[...])
    loads[3].wait()
    gate_part = mm(tokens[pl.ds(0, ROWS), :], w_in[0])
    head_part = mm(tokens[pl.ds(0, ROWS), :], w_in[1])
    lane = iota((ROWS, 128), 1)
    size_row = iota((16, 128), 0)
    for h in range(4):
        gate_half = gate_part[:, 128 * (h // 2):128 * (h // 2) + 128]
        head_half = head_part[:, 128 * (h // 2):128 * (h // 2) + 128]
        if h % 2 == 0:
            both = jnp.where(lane < 64, gate_half, pltpu.roll(head_half, 64, 1))
        else:
            both = jnp.where(lane < 64, pltpu.roll(gate_half, 64, 1), head_half)
        rs_src[h, pl.ds(0, ROWS), :] = both.astype(BF16)
        piece = jnp.zeros((16, 128), F32)
        for b in range(3):
            piece = jnp.where(size_row == b, sizes[h:h + 1, 128 * b:128 * b + 128], piece)
        rs_src[h, pl.ds(ROWS, 16), :] = piece.astype(BF16)

    for i in range(8):
        @pl.when(quarter * 8 + i != tp)
        def _():
            pltpu.make_async_copy(a_dst.at[i], a_dst.at[i], a_recv.at[i]).wait()
    own_maps = a_dst[...].astype(F32).reshape(64, PADDED)
    b_src[...] = own_maps.astype(BF16)
    b_copies = [
        pltpu.make_async_remote_copy(
            src_ref=b_src, dst_ref=b_dst.at[d - 1],
            send_sem=b_send.at[d - 1], recv_sem=b_recv.at[d - 1],
            device_id=device((samp + d) % 4, tp), device_id_type=MESH,
        )
        for d in range(1, 4)
    ]
    for copy in b_copies:
        copy.start()
    rs_copies = [
        pltpu.make_async_remote_copy(
            src_ref=rs_src.at[(samp + d) % 4], dst_ref=rs_dst.at[d - 1],
            send_sem=rs_send.at[d - 1], recv_sem=rs_recv.at[d - 1],
            device_id=device((samp + d) % 4, tp), device_id_type=MESH,
        )
        for d in range(1, 4)
    ]
    for copy in rs_copies:
        copy.start()

    total = own_maps
    for d in range(3):
        b_copies[d].wait_recv()
        total = total + b_dst[d].astype(F32)
    total = total.astype(BF16).astype(F32)
    taps = [own_maps[:, 320 + k:321 + k] + own_maps[:, 328 + k:329 + k] for k in range(5)]
    before = total[:, :PROMPT]
    lane_p = iota((64, PROMPT), 1)
    conv = taps[4] + taps[3] * before
    for k in range(1, 4):
        conv = conv + taps[3 - k] * jnp.where(lane_p >= k, pltpu.roll(before, k, 1), 0.0)
    maps_prompt = silu(conv).astype(BF16)
    lane_f = iota((64, 128), 1)
    line = pltpu.roll(total[:, PROMPT:], 48, 1)
    for k in range(3):
        line = jnp.where(
            jnp.logical_and(lane_f >= 16 * k, lane_f < 16 * k + 16), before[:, 253 + k:254 + k], line
        )
    conv = taps[4] + taps[0] * line
    for k in range(1, 4):
        conv = conv + taps[k] * pltpu.roll(line, 128 - 16 * k, 1)
    maps_fresh = jnp.where(lane_f < 64, silu(conv), 0.0).astype(BF16)
    maps[quarter, :, pl.ds(0, PROMPT)] = maps_prompt
    maps[quarter, :, pl.ds(PROMPT, 128)] = maps_fresh
    c_copies = [
        pltpu.make_async_remote_copy(
            src_ref=maps.at[quarter], dst_ref=maps.at[quarter],
            send_sem=c_send.at[d - 1], recv_sem=c_recv.at[d - 1],
            device_id=device(samp, group * 4 + (quarter + d) % 4), device_id_type=MESH,
        )
        for d in range(1, 4)
    ]
    for copy in c_copies:
        copy.start()

    summed = rs_src[samp].astype(F32)
    for d in range(3):
        rs_copies[d].wait_recv()
        summed = summed + rs_dst[d].astype(F32)
    summed = summed.astype(BF16).astype(F32)
    lane128 = iota((1, 128), 1)

    def of_head(value):
        chosen = jnp.zeros((value.shape[0], 128), F32)
        for h in range(4):
            half = value[:, 128 * (h // 2):128 * (h // 2) + 128]
            if h % 2 == 0:
                half = pltpu.roll(half, 64, 1)
            chosen = jnp.where(samp == h, half, chosen)
        return jnp.where(lane128 >= 64, chosen, 0.0)

    taps8 = of_head(jnp.concatenate([taps_ref[...], bias_ref[...], jnp.zeros((3, CHANNELS), F32)], axis=0))
    before = summed[:PROMPT]
    row_p = iota((PROMPT, 128), 0)
    conv = taps8[4:5] + taps8[3:4] * before
    for k in range(1, 4):
        conv = conv + taps8[3 - k:4 - k] * jnp.where(row_p >= k, pltpu.roll(before, k, 0), 0.0)
    mixed[pl.ds(0, PROMPT), :] = silu(conv).astype(BF16)
    line = jnp.concatenate(
        [jnp.broadcast_to(before[253 + k:254 + k], (16, 128)) for k in range(3)] + [summed[PROMPT:ROWS]], axis=0
    )
    conv = taps8[4:5] + taps8[0:1] * line[0:64]
    for k in range(1, 4):
        conv = conv + taps8[k:k + 1] * line[16 * k:16 * k + 64]
    mixed[pl.ds(PROMPT, FRESH), :] = silu(conv).astype(BF16)
    mixed[pl.ds(ROWS, PADDED - ROWS), :] = jnp.zeros((PADDED - ROWS, 128), BF16)

    size = jnp.concatenate([summed[ROWS + b:ROWS + b + 1] for b in range(3)], axis=1)
    size = jnp.broadcast_to(size, (8, PADDED)) + step_bias_ref[samp]
    size = jnp.maximum(size, 0.0) + jnp.log1p(jnp.exp(-jnp.abs(size)))
    rate = jnp.exp(jnp.full((8, PADDED), decay_ref[samp], F32))
    logs = -size * rate
    run = logs[:, :PROMPT]
    lane_r = iota((8, PROMPT), 1)
    for k in (1, 2, 4, 8, 16, 32, 64, 128):
        run = run + jnp.where(lane_r >= k, pltpu.roll(run, k, 1), 0.0)
    run_f = logs[:, PROMPT:]
    lane_s = iota((8, 128), 1)
    for k in (16, 32):
        run_f = run_f + jnp.where(lane_s >= k, pltpu.roll(run_f, k, 1), 0.0)
    run_f = run_f + run[:, PROMPT - 1:PROMPT]
    runs = [run[0:1, 0:128], run[0:1, 128:256], run_f[0:1]]
    trail = jnp.concatenate([jnp.transpose(jnp.broadcast_to(r, (128, 128))) for r in runs], axis=0)[:ROWS]

    for copy in c_copies:
        copy.wait_recv()
    to_read = jnp.concatenate([maps[2], maps[3]], axis=0).astype(F32)
    readout = jnp.transpose(to_read)[:ROWS].astype(BF16)
    inputs = jnp.concatenate([maps[0], maps[1]], axis=0)
    row_q = iota((ROWS, 128), 0)
    reading = skip_ref[samp] * mixed[pl.ds(0, ROWS), :].astype(F32)
    for b in range(3):
        products = mm(readout, inputs[:, 128 * b:128 * b + 128])
        if b < 2:
            seen = lane + 128 * b <= row_q
        else:
            seen = jnp.logical_and(lane <= row_q - PROMPT, lane % 16 == row_q % 16)
        gap = jnp.where(seen, trail - runs[b], -1e30)
        weight = jnp.exp(gap) * size[0:1, 128 * b:128 * b + 128] * products
        reading = reading + mm(weight.astype(BF16), mixed[pl.ds(128 * b, 128), :])

    gate = pltpu.roll(summed[:ROWS], 64, 1)
    gated = reading * silu(gate)
    fresh = mm(requarter, gated[PROMPT:].astype(BF16))
    blocks = [jnp.concatenate([gated[64 * i:64 * i + 64], fresh[16 * i:16 * i + 16]], axis=0) for i in range(4)]
    upper = jnp.concatenate(blocks[:2], axis=0)
    lower = jnp.concatenate(blocks[2:], axis=0)
    lane_h = iota((160, 128), 1)
    gat[samp] = jnp.where(lane_h < 64, pltpu.roll(upper, 64, 1), lower).astype(BF16)
    g_copies = [
        pltpu.make_async_remote_copy(
            src_ref=gat.at[samp], dst_ref=gat.at[samp],
            send_sem=g_send.at[d - 1], recv_sem=g_recv.at[d - 1],
            device_id=device((samp + d) % 4, tp), device_id_type=MESH,
        )
        for d in range(1, 4)
    ]
    for copy in g_copies:
        copy.start()
    for copy in g_copies:
        copy.wait_recv()
    for pair in range(2):
        first, second = gat[2 * pair].astype(F32), gat[2 * pair + 1].astype(F32)
        columns = pl.ds(128 * pair, 128)
        wide[pl.ds(0, 160), columns] = jnp.where(lane_h < 64, first, pltpu.roll(second, 64, 1))
        wide[pl.ds(160, 160), columns] = jnp.where(lane_h < 64, pltpu.roll(first, 64, 1), second)

    squares = jnp.sum(wide[pl.ds(0, ROWS), :] * wide[pl.ds(0, ROWS), :], axis=1, keepdims=True)
    squares = jnp.concatenate([squares, jnp.zeros((PADDED - ROWS, 1), F32)], axis=0)
    squares = jnp.transpose(jnp.broadcast_to(squares, (PADDED, 128)))[0:8]
    sq_src[...] = squares
    q_copies = [
        pltpu.make_async_remote_copy(
            src_ref=sq_src, dst_ref=sq_dst.at[d - 1],
            send_sem=q_send.at[d - 1], recv_sem=q_recv.at[d - 1],
            device_id=device(samp, group * 4 + (quarter + d) % 4), device_id_type=MESH,
        )
        for d in range(1, 4)
    ]
    for copy in q_copies:
        copy.start()
    for d in range(3):
        q_copies[d].wait_recv()
        squares = squares + sq_dst[d]
    scale = lax.rsqrt(squares * (1.0 / 1024.0) + 1e-5)
    scale = jnp.transpose(jnp.broadcast_to(scale[0:1], (128, PADDED)))[:ROWS]
    for half in range(2):
        columns = pl.ds(128 * half, 128)
        normed[:, columns] = (wide[pl.ds(0, ROWS), columns] * scale * gain_ref[:, columns]).astype(BF16)

    loads[4].wait()

    def d1_copy(i):
        return pltpu.make_async_remote_copy(
            src_ref=d1_src.at[i], dst_ref=d1_dst.at[i],
            send_sem=d1_send.at[i], recv_sem=d1_recv.at[i],
            device_id=device(samp, low * 8 + across * 2 + 1 - core), device_id_type=MESH,
        )

    for i in range(4):
        columns = pl.ds(pl.multiple_of((2 * i + 1 - core) * 256, 256), 256)
        d1_src[i] = mm(normed[...], w_out[:, columns]).astype(BF16)
        d1_copy(i).start()
    for i in range(4):
        columns = pl.ds(pl.multiple_of((2 * i + core) * 256, 256), 256)
        own[i] = mm(normed[...], w_out[:, columns])
    for i in range(4):
        d1_copy(i).wait_recv()

    def d2_copy(d, s):
        return pltpu.make_async_remote_copy(
            src_ref=d2_src.at[d - 1, s], dst_ref=d2_dst.at[d - 1, s],
            send_sem=d2_send.at[d - 1, s], recv_sem=d2_recv.at[d - 1, s],
            device_id=device(samp, low * 8 + ((across + d) % 4) * 2 + core), device_id_type=MESH,
        )

    for s in range(4):
        rows = pl.ds(BLOCK * s, BLOCK)
        for d in range(1, 4):
            to = (across + d) % 4
            d2_src[d - 1, s] = (own[to, rows, :] + d1_dst[to, rows, :].astype(F32)).astype(BF16)
            d2_copy(d, s).start()

    def d3_copy(s):
        return pltpu.make_async_remote_copy(
            src_ref=d3_src.at[s], dst_ref=d3_dst.at[low],
            send_sem=d3_send.at[s], recv_sem=d3_recv.at[low],
            device_id=device(s, samp * 8 + place), device_id_type=MESH,
        )

    def stays(s):
        return jnp.logical_and(samp == low, samp == s)

    for s in range(4):
        rows = pl.ds(BLOCK * s, BLOCK)
        value = own[across, rows, :] + d1_dst[across, rows, :].astype(F32)
        for d in range(1, 4):
            d2_copy(d, s).wait_recv()
            value = value + d2_dst[d - 1, s].astype(F32)
        d3_src[s] = value.astype(BF16)

        @pl.when(stays(s))
        def _():
            d3_dst[low] = d3_src[s]

        @pl.when(jnp.logical_not(stays(s)))
        def _():
            d3_copy(s).start()

    for i in range(4):
        @pl.when(jnp.logical_or(low != samp, i != low))
        def _():
            pltpu.make_async_copy(d3_dst.at[i], d3_dst.at[i], d3_recv.at[i]).wait()
    value = d3_dst[0].astype(F32)
    for i in range(1, 4):
        value = value + d3_dst[i].astype(F32)
    prefill_ref[...] = value[:64].astype(BF16)
    decode_ref[...] = value[64:].astype(BF16)

    for g in range(8):
        @pl.when(g * 4 + low != tp)
        def _():
            a_copy(g).wait_send()
    for copy in b_copies + rs_copies + c_copies + g_copies + q_copies:
        copy.wait_send()
    for i in range(4):
        d1_copy(i).wait_send()
    for s in range(4):
        for d in range(1, 4):
            d2_copy(d, s).wait_send()

        @pl.when(jnp.logical_not(stays(s)))
        def _():
            d3_copy(s).wait_send()


def shards(
    prompt_tokens, step_tokens, lengths, input_weight, group_weight, step_weight,
    conv_weight, group_conv, conv_bias, group_bias, step_bias, decay_log, skip_gain, norm_gain, output_weight,
):
    anywhere = pl.BlockSpec(memory_space=pl.ANY)
    vector = pl.BlockSpec(memory_space=pltpu.VMEM)
    scalar = pl.BlockSpec(memory_space=pltpu.SMEM)
    dma = pltpu.SemaphoreType.DMA
    prefill, decode = pl.pallas_call(
        kernel,
        out_shape=(
            jax.ShapeDtypeStruct((64, CHANNELS), BF16),
            jax.ShapeDtypeStruct((16, CHANNELS), BF16),
        ),
        in_specs=[anywhere] * 5 + [vector] * 5 + [scalar] * 3 + [vector],
        out_specs=(vector, vector),
        scratch_shapes=[
            pltpu.VMEM((PADDED, WIDTH), BF16),
            pltpu.VMEM((2, WIDTH, CHANNELS), BF16),
            pltpu.VMEM((64, WIDTH), BF16),
            pltpu.VMEM((CHANNELS, WIDTH), BF16),
            dma((5,)),
            pltpu.VMEM((128, 64), F32),
            pltpu.VMEM((8, 8, PADDED), BF16),
            pltpu.VMEM((8, 8, PADDED), BF16),
            pltpu.VMEM((64, PADDED), BF16),
            pltpu.VMEM((3, 64, PADDED), BF16),
            pltpu.VMEM((4, 64, PADDED), BF16),
            pltpu.VMEM((4, MSG, 128), BF16),
            pltpu.VMEM((3, MSG, 128), BF16),
            pltpu.VMEM((PADDED, 128), BF16),
            pltpu.VMEM((4, 160, 128), BF16),
            pltpu.VMEM((ROWS, CHANNELS), F32),
            pltpu.VMEM((8, PADDED), F32),
            pltpu.VMEM((3, 8, PADDED), F32),
            pltpu.VMEM((ROWS, CHANNELS), BF16),
            pltpu.VMEM((4, ROWS, CHANNELS), BF16),
            pltpu.VMEM((4, ROWS, CHANNELS), BF16),
            pltpu.VMEM((4, ROWS, CHANNELS), F32),
            pltpu.VMEM((3, 4, BLOCK, CHANNELS), BF16),
            pltpu.VMEM((3, 4, BLOCK, CHANNELS), BF16),
            pltpu.VMEM((4, BLOCK, CHANNELS), BF16),
            pltpu.VMEM((4, BLOCK, CHANNELS), BF16),
            dma((8,)), dma((8,)), dma((3,)), dma((3,)), dma((3,)), dma((3,)), dma((3,)), dma((3,)),
            dma((3,)), dma((3,)), dma((3,)), dma((3,)), dma((4,)), dma((4,)),
            dma((3, 4)), dma((3, 4)), dma((4,)), dma((4,)),
        ],
        compiler_params=pltpu.CompilerParams(
            collective_id=0, has_side_effects=True, vmem_limit_bytes=40 * 1024 * 1024
        ),
        cost_estimate=pl.CostEstimate(flops=2 * 10**9, bytes_accessed=8 * 10**6, transcendentals=10**6),
    )(
        prompt_tokens.reshape(PROMPT, WIDTH),
        step_tokens.reshape(FRESH, WIDTH),
        input_weight,
        group_weight.T,
        output_weight,
        step_weight.T,
        conv_weight,
        conv_bias.reshape(1, CHANNELS),
        group_conv,
        group_bias.reshape(1, 64),
        step_bias,
        decay_log,
        skip_gain,
        norm_gain.reshape(1, CHANNELS),
    )
    active = jnp.arange(4)[:, None, None] < lengths[None]
    decode = decode.reshape(4, 4, 1, CHANNELS)
    return prefill.reshape(64, 1, CHANNELS), jnp.where(active[..., None], decode, jnp.zeros_like(decode))


def solution(mesh):
    placed = (
        P(None, "rep", "samp"),
        P(None, None, "rep", "samp"),
        P("samp", "rep"),
        P(None, "samp", "tp"),
        P("samp", "tp"),
        P("samp", "tp"),
        P(None, "tp"),
        P(None, "tp"),
        P("tp"),
        P("tp"),
        P("tp"),
        P("tp"),
        P("tp"),
        P("tp"),
        P("tp", "samp"),
    )
    return jax.shard_map(
        shards,
        mesh=mesh,
        in_specs=placed,
        out_specs=(P("samp", "rep", "tp"), P(None, "samp", "rep", "tp")),
        check_vma=False,
    )
```

```python
import jax
import jax.numpy as jnp
from jax import lax
from jax.experimental import pallas as pl
from jax.experimental.pallas import tpu as pltpu
from jax.sharding import PartitionSpec as P

PROMPT = 256
FRESH = 64
ROWS = 320
PADDED = 384
WIDTH = 2048
CHANNELS = 256
BLOCK = 80
VMEM_LIMIT = 60 * 1024 * 1024
MESH = pl.DeviceIdType.MESH
F32 = jnp.float32
BF16 = jnp.bfloat16
NT = (((1,), (1,)), ((), ()))


def mm(a, b):
    return jnp.dot(a, b, preferred_element_type=F32)


def mm_nt(a, b):
    return lax.dot_general(a, b, NT, preferred_element_type=F32)


def iota(shape, axis):
    return lax.broadcasted_iota(jnp.int32, shape, axis)


def silu(v):
    return v / (1.0 + jnp.exp(-v))


def kernel(
    prompt_ref, fresh_ref, in_ref, group_ref, out_ref, step_ref, taps_ref, bias_ref,
    group_taps_ref, group_bias_ref, step_bias_ref, decay_ref, skip_ref, gain_ref,
    prefill_ref, decode_ref,
    tokens, w_in, w_group, w_out, w_step, taps_v, bias_v, group_taps_v, group_bias_v,
    step_bias_v, decay_v, skip_v, gain_v, load_sem,
    packed_taps, a_src, a_dst, b_src, b_dst, maps, x_src, x_dst, z_src, z_dst,
    mixed, weights, gat, wide, sq_src, sq_dst, unscaled,
    d1_src, d1_dst, own, d2_src, d2_dst, d3_src, d3_dst,
    a_send, a_recv, b_send, b_recv, c_send, c_recv, x_send, x_recv, z_send, z_recv,
    g_send, g_recv, q_send, q_recv, d1_send, d1_recv, d2_send, d2_recv, d3_send, d3_recv,
):
    rep = lax.axis_index("rep")
    samp = lax.axis_index("samp")
    tp = lax.axis_index("tp")
    low = tp // 8
    place = tp % 8
    across = place // 2
    core = place % 2
    group = tp // 4
    quarter = tp % 4

    def device(samp_index, tp_index):
        return (rep, samp_index, tp_index)

    barrier = pltpu.get_barrier_semaphore()

    def greet(samp_index, tp_index):
        pl.semaphore_signal(barrier, inc=1, device_id=device(samp_index, tp_index), device_id_type=MESH)

    for d in (2, 1, 3):
        greet((samp + d) % 4, tp)
    for i in range(4):
        @pl.when(jnp.logical_or(low != samp, i != low))
        def _():
            greet(low, i * 8 + place)
    for i in range(8):
        @pl.when(quarter * 8 + i != tp)
        def _():
            greet(samp, quarter * 8 + i)
    for d in range(1, 4):
        greet(samp, group * 4 + (quarter + d) % 4)
        greet(samp, low * 8 + ((across + d) % 4) * 2 + core)

    pairs = (
        (group_ref, w_group), (prompt_ref, tokens.at[pl.ds(0, PROMPT)]), (fresh_ref, tokens.at[pl.ds(PROMPT, FRESH)]),
        (group_taps_ref, group_taps_v), (group_bias_ref, group_bias_v), (step_ref, w_step),
        (in_ref.at[1], w_in.at[1]), (in_ref.at[0], w_in.at[0]), (taps_ref, taps_v), (bias_ref, bias_v),
        (step_bias_ref, step_bias_v), (decay_ref, decay_v), (skip_ref, skip_v), (gain_ref, gain_v), (out_ref, w_out),
    )
    loads = [pltpu.make_async_copy(a, b, load_sem.at[i]) for i, (a, b) in enumerate(pairs)]
    for load in loads:
        load.start()
    sends = []

    def copy(source, target, send, recv, samp_index, tp_index):
        return pltpu.make_async_remote_copy(
            src_ref=source, dst_ref=target, send_sem=send, recv_sem=recv,
            device_id=device(samp_index, tp_index), device_id_type=MESH,
        )

    def start(copies):
        for one in copies:
            one.start()
            sends.append(one)
        return copies

    tokens[pl.ds(ROWS, PADDED - ROWS), :] = jnp.zeros((PADDED - ROWS, WIDTH), BF16)
    packed_taps[...] = jnp.zeros(packed_taps.shape, F32)
    mixed[pl.ds(ROWS, PADDED - ROWS), :] = jnp.zeros((PADDED - ROWS, 128), BF16)

    row = iota((64, 64), 0)
    col = iota((64, 64), 1)
    regroup = (col == (row % 8) * 8 + row // 8).astype(F32).astype(BF16)
    requarter = (col == ((row % 16) // 4) * 16 + (row // 16) * 4 + row % 4).astype(F32).astype(BF16)

    for load in loads[:5]:
        load.wait()
    for at, value in ((64, group_taps_v[...]), (68, group_bias_v[...])):
        high = value.astype(BF16).astype(F32)
        packed_taps[pl.ds(at, value.shape[0]), :] = high
        packed_taps[pl.ds(at + 8, value.shape[0]), :] = value - high
    maps_partial = mm_nt(w_group[...], tokens[...]).astype(BF16)
    regrouped = mm(regroup, maps_partial)
    tail = regrouped[:, PROMPT:] + mm_nt(regroup, packed_taps[...].astype(BF16))
    a_src[:, :, pl.ds(0, PROMPT)] = regrouped[:, :PROMPT].reshape(8, 8, PROMPT).astype(BF16)
    a_src[:, :, pl.ds(PROMPT, 128)] = tail.reshape(8, 8, 128).astype(BF16)

    pl.semaphore_wait(
        barrier, 19 + jnp.where(quarter != low, 1, 0) + jnp.where(samp != low, 1, 0)
    )

    def a_copy(g):
        return copy(a_src.at[g], a_dst.at[place], a_send.at[g], a_recv.at[place], samp, g * 4 + low)

    for g in range(8):
        @pl.when(g * 4 + low != tp)
        def _():
            a_copy(g).start()

        @pl.when(g * 4 + low == tp)
        def _():
            a_dst[pl.ds(place, 1)] = a_src[pl.ds(g, 1)]

    lane_h = iota((160, 128), 1)

    def packed(part, h):
        upper = part[:160, 128 * (h // 2):128 * (h // 2) + 128]
        lower = part[160:, 128 * (h // 2):128 * (h // 2) + 128]
        if h % 2 == 0:
            return jnp.where(lane_h < 64, upper, pltpu.roll(lower, 64, 1)).astype(BF16)
        return jnp.where(lane_h < 64, pltpu.roll(upper, 64, 1), lower).astype(BF16)

    def to_heads(source, target, send, recv):
        return [
            copy(source.at[(samp + d) % 4], target.at[d - 1], send.at[d - 1], recv.at[d - 1], (samp + d) % 4, tp)
            for d in (2, 1, 3)
        ]

    loads[5].wait()
    sizes = mm_nt(w_step[...], tokens[...])
    loads[6].wait()
    head_part = mm(tokens[pl.ds(0, ROWS), :], w_in[1])
    size_row = iota((16, 128), 0)
    for h in range(4):
        x_src[h, pl.ds(0, 160), :] = packed(head_part, h)
        piece = jnp.zeros((16, 128), F32)
        for b in range(3):
            piece = jnp.where(size_row == b, sizes[h:h + 1, 128 * b:128 * b + 128], piece)
        x_src[h, pl.ds(160, 16), :] = piece.astype(BF16)
    x_copies = start(to_heads(x_src, x_dst, x_send, x_recv))
    loads[7].wait()
    gate_part = mm(tokens[pl.ds(0, ROWS), :], w_in[0])
    for h in range(4):
        z_src[h] = packed(gate_part, h)

    for i in range(8):
        @pl.when(quarter * 8 + i != tp)
        def _():
            pltpu.make_async_copy(a_dst.at[i], a_dst.at[i], a_recv.at[i]).wait()
    own_maps = a_dst[...].astype(F32).reshape(64, PADDED)
    lane_q = iota((32, 128), 1)
    fresh_maps = own_maps[:, PROMPT:]
    b_src[pl.ds(0, 64), :] = own_maps[:, 0:128].astype(BF16)
    b_src[pl.ds(64, 64), :] = own_maps[:, 128:256].astype(BF16)
    b_src[pl.ds(128, 32), :] = jnp.where(lane_q < 64, fresh_maps[:32], pltpu.roll(fresh_maps[32:], 64, 1)).astype(BF16)
    b_copies = start([
        copy(b_src, b_dst.at[d - 1], b_send.at[d - 1], b_recv.at[d - 1], (samp + d) % 4, tp) for d in (2, 1, 3)
    ])
    for one in b_copies:
        one.wait_send()
    z_copies = start(to_heads(z_src, z_dst, z_send, z_recv))

    lane128 = iota((1, 128), 1)

    def of_head(value):
        chosen = jnp.zeros((value.shape[0], 128), F32)
        for h in range(4):
            half = value[:, 128 * (h // 2):128 * (h // 2) + 128]
            if h % 2 == 0:
                half = pltpu.roll(half, 64, 1)
            chosen = jnp.where(samp == h, half, chosen)
        return jnp.where(lane128 >= 64, chosen, 0.0)

    def own_scalar(ref):
        return jnp.sum(jnp.where(iota((1, 4), 1) == samp, ref[...], 0.0), axis=1, keepdims=True)

    def unpacked(value):
        return jnp.concatenate([pltpu.roll(value, 64, 1), value], axis=0)

    for load in loads[8:13]:
        load.wait()
    taps8 = of_head(jnp.concatenate([taps_v[...], bias_v[...], jnp.zeros((3, CHANNELS), F32)], axis=0))
    skip = own_scalar(skip_v)
    step_bias = own_scalar(step_bias_v)
    rate = jnp.exp(own_scalar(decay_v))
    for one in x_copies:
        one.wait_recv()
    summed = x_src[samp].astype(F32)
    for d in range(3):
        summed = summed + x_dst[d].astype(F32)
    summed = summed.astype(BF16).astype(F32)
    heads = unpacked(summed[:160])
    before = heads[:PROMPT]
    row_p = iota((PROMPT, 128), 0)
    conv = taps8[4:5] + taps8[3:4] * before
    for k in range(1, 4):
        conv = conv + taps8[3 - k:4 - k] * jnp.where(row_p >= k, pltpu.roll(before, k, 0), 0.0)
    mixed[pl.ds(0, PROMPT), :] = silu(conv).astype(BF16)
    line = jnp.concatenate(
        [jnp.broadcast_to(before[253 + k:254 + k], (16, 128)) for k in range(3)] + [heads[PROMPT:ROWS]], axis=0
    )
    conv = taps8[4:5] + taps8[0:1] * line[0:64]
    for k in range(1, 4):
        conv = conv + taps8[k:k + 1] * line[16 * k:16 * k + 64]
    mixed[pl.ds(PROMPT, FRESH), :] = silu(conv).astype(BF16)

    size = jnp.concatenate([summed[160 + b:161 + b] for b in range(3)], axis=1)
    size = jnp.broadcast_to(size, (8, PADDED)) + step_bias
    size = jnp.maximum(size, 0.0) + jnp.log1p(jnp.exp(-jnp.abs(size)))
    logs = -size * rate
    run = logs[:, :PROMPT]
    lane_r = iota((8, PROMPT), 1)
    for k in (1, 2, 4, 8, 16, 32, 64, 128):
        run = run + jnp.where(lane_r >= k, pltpu.roll(run, k, 1), 0.0)
    run_f = logs[:, PROMPT:]
    lane_s = iota((8, 128), 1)
    for k in (16, 32):
        run_f = run_f + jnp.where(lane_s >= k, pltpu.roll(run_f, k, 1), 0.0)
    run_f = run_f + run[:, PROMPT - 1:PROMPT]
    runs = [run[0:1, 0:128], run[0:1, 128:256], run_f[0:1]]
    trail = jnp.concatenate([jnp.transpose(jnp.broadcast_to(r, (128, 128))) for r in runs], axis=0)[:ROWS]
    lane = iota((128, 128), 1)
    row_q = iota((128, 128), 0)
    tiles = ((256, 64, 0), (256, 64, 1), (256, 64, 2), (0, 128, 0), (128, 128, 0), (128, 128, 1))
    offsets = (0, 64, 128, 192, 320, 448)
    for (first, count, b), offset in zip(tiles, offsets):
        gap = trail[first:first + count] - runs[b]
        if b == 2:
            seen = jnp.logical_and(lane <= row_q, lane % 16 == row_q % 16)[:count]
            gap = jnp.where(seen, gap, -1e30)
        elif first == 128 * b:
            gap = jnp.where(lane <= row_q, gap, -1e30)
        weights[pl.ds(offset, count), :] = jnp.exp(gap) * size[0:1, 128 * b:128 * b + 128]

    for one in b_copies:
        one.wait_recv()
    total = b_src[...].astype(F32)
    for d in range(3):
        total = total + b_dst[d].astype(F32)
    total = total.astype(BF16).astype(F32)
    taps = [own_maps[:, 320 + k:321 + k] + own_maps[:, 328 + k:329 + k] for k in range(5)]
    before = jnp.concatenate([total[0:64], total[64:128]], axis=1)
    lane_p = iota((64, PROMPT), 1)
    conv = taps[4] + taps[3] * before
    for k in range(1, 4):
        conv = conv + taps[3 - k] * jnp.where(lane_p >= k, pltpu.roll(before, k, 1), 0.0)
    maps_prompt = silu(conv).astype(BF16)
    lane_f = iota((64, 128), 1)
    line = jnp.concatenate([total[128:160], pltpu.roll(total[128:160], 64, 1)], axis=0)
    line = pltpu.roll(line, 48, 1)
    for k in range(3):
        line = jnp.where(
            jnp.logical_and(lane_f >= 16 * k, lane_f < 16 * k + 16), before[:, 253 + k:254 + k], line
        )
    conv = taps[4] + taps[0] * line
    for k in range(1, 4):
        conv = conv + taps[k] * pltpu.roll(line, 128 - 16 * k, 1)
    maps_fresh = jnp.where(lane_f < 64, silu(conv), 0.0).astype(BF16)
    maps[quarter, :, pl.ds(0, PROMPT)] = maps_prompt
    maps[quarter, :, pl.ds(PROMPT, 128)] = maps_fresh
    c_copies = start([
        copy(maps.at[quarter], maps.at[quarter], c_send.at[d - 1], c_recv.at[d - 1], samp, group * 4 + (quarter + d) % 4)
        for d in (3, 2, 1)
    ])
    for one in c_copies:
        one.wait_recv()
    inputs = jnp.concatenate([maps[0], maps[1]], axis=0)
    to_read = jnp.concatenate([maps[2], maps[3]], axis=0).astype(F32)
    readout = jnp.transpose(to_read).astype(BF16)

    def read(first, count, blocks):
        value = skip * mixed[pl.ds(first, count), :].astype(F32)
        for b, offset in blocks:
            products = mm(readout[first:first + count], inputs[:, 128 * b:128 * b + 128])
            seen = (weights[pl.ds(offset, count), :] * products).astype(BF16)
            value = value + mm(seen, mixed[pl.ds(128 * b, 128), :])
        return value

    fresh = read(256, 64, ((0, 0), (1, 64), (2, 128)))
    halves = [read(0, 128, ((0, 192),)), read(128, 128, ((0, 320), (1, 448)))]
    for one in z_copies:
        one.wait_recv()
    gate = z_src[samp].astype(F32)
    for d in range(3):
        gate = gate + z_dst[d].astype(F32)
    gate = silu(unpacked(gate.astype(BF16).astype(F32)))
    fresh = mm(requarter, (fresh * gate[PROMPT:]).astype(BF16))

    lane_c = iota((BLOCK, 128), 1)
    g_copies = []
    for c in range(2):
        gated = halves[c] * gate[128 * c:128 * c + 128]
        upper = jnp.concatenate([gated[:64], fresh[32 * c:32 * c + 16]], axis=0)
        lower = jnp.concatenate([gated[64:], fresh[32 * c + 16:32 * c + 32]], axis=0)
        gat[c, samp] = jnp.where(lane_c < 64, pltpu.roll(upper, 64, 1), lower).astype(BF16)
        g_copies.append(start([
            copy(gat.at[c, samp], gat.at[c, samp], g_send.at[c, d - 1], g_recv.at[c, d - 1], (samp + d) % 4, tp)
            for d in (2, 1, 3)
        ]))

    for load in loads[13:]:
        load.wait()

    def d1_copy(c, i):
        return copy(
            d1_src.at[c, i], d1_dst.at[c, i], d1_send.at[c, i], d1_recv.at[c, i],
            samp, low * 8 + across * 2 + 1 - core,
        )

    def d2_copy(d, s):
        return copy(
            d2_src.at[d - 1, s], d2_dst.at[d - 1, s], d2_send.at[d - 1, s], d2_recv.at[d - 1, s],
            samp, low * 8 + ((across + d) % 4) * 2 + core,
        )

    def d3_copy(s):
        return copy(d3_src.at[s], d3_dst.at[low], d3_send.at[s], d3_recv.at[low], s, samp * 8 + place)

    for c in range(2):
        for one in g_copies[c]:
            one.wait_recv()
        for pair in range(2):
            first, second = gat[c, 2 * pair].astype(F32), gat[c, 2 * pair + 1].astype(F32)
            columns = pl.ds(128 * pair, 128)
            wide[pl.ds(0, BLOCK), columns] = jnp.where(lane_c < 64, first, pltpu.roll(second, 64, 1))
            wide[pl.ds(BLOCK, BLOCK), columns] = jnp.where(lane_c < 64, pltpu.roll(first, 64, 1), second)
        gathered = wide[...]
        unscaled[...] = (gathered * gain_v[...]).astype(BF16)

        squares = jnp.sum(gathered * gathered, axis=1, keepdims=True)
        squares = jnp.concatenate([squares, jnp.zeros((96, 1), F32)], axis=0)
        squares = jnp.transpose(jnp.broadcast_to(squares, (256, 128)))[0:8]
        sq_src[c] = squares
        q_copies = start([
            copy(
                sq_src.at[c], sq_dst.at[c, d - 1], q_send.at[c, d - 1], q_recv.at[c, d - 1],
                samp, group * 4 + (quarter + d) % 4,
            )
            for d in (3, 2, 1)
        ])

        d1_copies = [d1_copy(c, i) for i in range(4)]
        for i in range(4):
            columns = pl.ds(pl.multiple_of((2 * i + 1 - core) * 256, 256), 256)
            d1_src[c, i] = mm(unscaled[...], w_out[:, columns]).astype(BF16)
            start([d1_copies[i]])
        for i in range(4):
            columns = pl.ds(pl.multiple_of((2 * i + core) * 256, 256), 256)
            own[i] = mm(unscaled[...], w_out[:, columns])
        for one in q_copies:
            one.wait_recv()
        for d in range(3):
            squares = squares + sq_dst[c, d]
        scale = lax.rsqrt(squares * (1.0 / 1024.0) + 1e-5)
        scale = jnp.transpose(jnp.broadcast_to(scale[0:1], (128, 256)))[:160]
        scale = jnp.concatenate([scale, scale], axis=1)
        for one in d1_copies:
            one.wait_recv()
        for half in range(2):
            s = 2 * c + half
            rows = pl.ds(BLOCK * half, BLOCK)
            by = scale[BLOCK * half:BLOCK * half + BLOCK]
            for d in (2, 1, 3):
                to = (across + d) % 4
                d2_src[d - 1, s] = ((own[to, rows, :] + d1_dst[c, to, rows, :].astype(F32)) * by).astype(BF16)
                start([d2_copy(d, s)])
            kept = (own[across, rows, :] + d1_dst[c, across, rows, :].astype(F32)) * by
            if s == 0:
                kept_all = [kept]
            else:
                kept_all.append(kept)

    def stays(s):
        return jnp.logical_and(samp == low, samp == s)

    for s in range(4):
        value = kept_all[s]
        for d in range(1, 4):
            d2_copy(d, s).wait_recv()
            value = value + d2_dst[d - 1, s].astype(F32)
        d3_src[s] = value.astype(BF16)

        @pl.when(stays(s))
        def _():
            d3_dst[low] = d3_src[s]

        @pl.when(jnp.logical_not(stays(s)))
        def _():
            d3_copy(s).start()

    for i in range(4):
        @pl.when(jnp.logical_or(low != samp, i != low))
        def _():
            pltpu.make_async_copy(d3_dst.at[i], d3_dst.at[i], d3_recv.at[i]).wait()
    value = d3_dst[0].astype(F32)
    for i in range(1, 4):
        value = value + d3_dst[i].astype(F32)
    prefill_ref[...] = value[:64].astype(BF16)
    decode_ref[...] = value[64:].astype(BF16)

    for g in range(8):
        @pl.when(g * 4 + low != tp)
        def _():
            a_copy(g).wait_send()
    for one in sends:
        if not any(one is other for other in b_copies):
            one.wait_send()
    for s in range(4):
        @pl.when(jnp.logical_not(stays(s)))
        def _():
            d3_copy(s).wait_send()


def shards(
    prompt_tokens, step_tokens, lengths, input_weight, group_weight, step_weight,
    conv_weight, group_conv, conv_bias, group_bias, step_bias, decay_log, skip_gain, norm_gain, output_weight,
):
    anywhere = pl.BlockSpec(memory_space=pl.ANY)
    vector = pl.BlockSpec(memory_space=pltpu.VMEM)

    def dma(*shape):
        return pltpu.SemaphoreType.DMA(shape)

    def room(*shape):
        return pltpu.VMEM(shape, BF16)

    def wide_room(*shape):
        return pltpu.VMEM(shape, F32)

    prefill, decode = pl.pallas_call(
        kernel,
        out_shape=(
            jax.ShapeDtypeStruct((64, CHANNELS), BF16),
            jax.ShapeDtypeStruct((16, CHANNELS), BF16),
        ),
        in_specs=[anywhere] * 14,
        out_specs=(vector, vector),
        scratch_shapes=[
            room(PADDED, WIDTH), room(2, WIDTH, CHANNELS), room(64, WIDTH), room(CHANNELS, WIDTH), room(4, WIDTH),
            wide_room(4, CHANNELS), wide_room(1, CHANNELS), wide_room(4, 64), wide_room(1, 64),
            wide_room(1, 4), wide_room(1, 4), wide_room(1, 4), wide_room(1, CHANNELS), dma(15),
            wide_room(128, 64),
            room(8, 8, PADDED), room(8, 8, PADDED),
            room(160, 128), room(3, 160, 128),
            room(4, 64, PADDED),
            room(4, 176, 128), room(3, 176, 128),
            room(4, 160, 128), room(3, 160, 128),
            room(PADDED, 128), wide_room(576, 128),
            room(2, 4, BLOCK, 128), wide_room(2 * BLOCK, CHANNELS),
            wide_room(2, 8, 256), wide_room(2, 3, 8, 256),
            room(2 * BLOCK, CHANNELS),
            room(2, 4, 2 * BLOCK, CHANNELS), room(2, 4, 2 * BLOCK, CHANNELS), wide_room(4, 2 * BLOCK, CHANNELS),
            room(3, 4, BLOCK, CHANNELS), room(3, 4, BLOCK, CHANNELS),
            room(4, BLOCK, CHANNELS), room(4, BLOCK, CHANNELS),
            dma(8), dma(8), dma(3), dma(3), dma(3), dma(3), dma(3), dma(3), dma(3), dma(3),
            dma(2, 3), dma(2, 3), dma(2, 3), dma(2, 3), dma(2, 4), dma(2, 4), dma(3, 4), dma(3, 4), dma(4), dma(4),
        ],
        compiler_params=pltpu.CompilerParams(
            collective_id=0, has_side_effects=True, vmem_limit_bytes=VMEM_LIMIT
        ),
        cost_estimate=pl.CostEstimate(flops=2 * 10**9, bytes_accessed=8 * 10**6, transcendentals=10**6),
    )(
        prompt_tokens.reshape(PROMPT, WIDTH),
        step_tokens.reshape(FRESH, WIDTH),
        input_weight,
        group_weight.T,
        output_weight,
        step_weight.T,
        conv_weight,
        conv_bias.reshape(1, CHANNELS),
        group_conv,
        group_bias.reshape(1, 64),
        step_bias.reshape(1, 4),
        decay_log.reshape(1, 4),
        skip_gain.reshape(1, 4),
        norm_gain.reshape(1, CHANNELS),
    )
    active = jnp.arange(4)[:, None, None] < lengths[None]
    decode = decode.reshape(4, 4, 1, CHANNELS)
    return prefill.reshape(64, 1, CHANNELS), jnp.where(active[..., None], decode, jnp.zeros_like(decode))


def solution(mesh):
    placed = (
        P(None, "rep", "samp"),
        P(None, None, "rep", "samp"),
        P("samp", "rep"),
        P(None, "samp", "tp"),
        P("samp", "tp"),
        P("samp", "tp"),
        P(None, "tp"),
        P(None, "tp"),
        P("tp"),
        P("tp"),
        P("tp"),
        P("tp"),
        P("tp"),
        P("tp"),
        P("tp", "samp"),
    )
    return jax.shard_map(
        shards,
        mesh=mesh,
        in_specs=placed,
        out_specs=(P("samp", "rep", "tp"), P(None, "samp", "rep", "tp")),
        check_vma=False,
    )
```

```python
import jax
import jax.numpy as jnp
from jax import lax
from jax.experimental import pallas as pl
from jax.experimental.pallas import tpu as pltpu
from jax.sharding import PartitionSpec as P

PROMPT = 256
FRESH = 64
ROWS = 320
PADDED = 384
WIDTH = 2048
CHANNELS = 256
BLOCK = 80
VMEM_LIMIT = 60 * 1024 * 1024
MESH = pl.DeviceIdType.MESH
F32 = jnp.float32
BF16 = jnp.bfloat16
NT = (((1,), (1,)), ((), ()))


def mm(a, b):
    return jnp.dot(a, b, preferred_element_type=F32)


def mm_nt(a, b):
    return lax.dot_general(a, b, NT, preferred_element_type=F32)


def iota(shape, axis):
    return lax.broadcasted_iota(jnp.int32, shape, axis)


def silu(v):
    return v / (1.0 + jnp.exp(-v))


def kernel(
    prompt_ref, fresh_ref, in_ref, group_ref, out_ref, step_ref, taps_ref, bias_ref,
    group_taps_ref, group_bias_ref, step_bias_ref, decay_ref, skip_ref, gain_ref,
    prefill_ref, decode_ref,
    tokens, w_in, w_group, w_out, w_step, taps_v, bias_v, group_taps_v, group_bias_v,
    step_bias_v, decay_v, skip_v, gain_v, load_sem,
    packed_taps, a_src, a_dst, b_src, b_dst, maps, x_src, x_dst, z_src, z_dst,
    w_src, w_all, mixed, weights, gat, gathered, sq_src, sq_dst,
    product, e_src, e_dst, d3_src, d3_dst,
    a_send, a_recv, b_send, b_recv, c_send, c_recv, x_send, x_recv, z_send, z_recv, w_send, w_recv,
    g_send, g_recv, f_send, f_recv, q_send, q_recv, e_send, e_recv, d3_send, d3_recv,
):
    rep = lax.axis_index("rep")
    samp = lax.axis_index("samp")
    tp = lax.axis_index("tp")
    low = tp // 8
    place = tp % 8
    across = place // 2
    core = place % 2
    group = tp // 4
    quarter = tp % 4

    def device(samp_index, tp_index):
        return (rep, samp_index, tp_index)

    pairs = (
        (group_ref, w_group), (prompt_ref, tokens.at[pl.ds(0, PROMPT)]), (fresh_ref, tokens.at[pl.ds(PROMPT, FRESH)]),
        (group_taps_ref, group_taps_v), (group_bias_ref, group_bias_v), (step_ref, w_step),
        (in_ref.at[1], w_in.at[1]), (in_ref.at[0], w_in.at[0]), (taps_ref, taps_v), (bias_ref, bias_v),
        (step_bias_ref, step_bias_v), (decay_ref, decay_v), (skip_ref, skip_v), (gain_ref, gain_v), (out_ref, w_out),
    )
    loads = [pltpu.make_async_copy(a, b, load_sem.at[i]) for i, (a, b) in enumerate(pairs)]
    for load in loads[:3]:
        load.start()

    barrier = pltpu.get_barrier_semaphore()

    def greet(samp_index, tp_index):
        pl.semaphore_signal(barrier, inc=1, device_id=device(samp_index, tp_index), device_id_type=MESH)

    for d in (2, 1, 3):
        greet((samp + d) % 4, tp)
    for i in range(4):
        @pl.when(jnp.logical_or(low != samp, i != low))
        def _():
            greet(low, i * 8 + place)
    for i in range(8):
        @pl.when(quarter * 8 + i != tp)
        def _():
            greet(samp, quarter * 8 + i)
    for d in range(1, 4):
        greet(samp, group * 4 + (quarter + d) % 4)
        greet(samp, low * 8 + ((across + d) % 4) * 2 + core)

    for load in loads[3:]:
        load.start()
    sends = []

    def copy(source, target, send, recv, samp_index, tp_index):
        return pltpu.make_async_remote_copy(
            src_ref=source, dst_ref=target, send_sem=send, recv_sem=recv,
            device_id=device(samp_index, tp_index), device_id_type=MESH,
        )

    def start(copies):
        for one in copies:
            one.start()
            sends.append(one)
        return copies

    tokens[pl.ds(ROWS, PADDED - ROWS), :] = jnp.zeros((PADDED - ROWS, WIDTH), BF16)
    packed_taps[...] = jnp.zeros(packed_taps.shape, F32)
    mixed[pl.ds(ROWS, PADDED - ROWS), :] = jnp.zeros((PADDED - ROWS, 128), BF16)

    row = iota((64, 64), 0)
    col = iota((64, 64), 1)
    regroup = (col == (row % 8) * 8 + row // 8).astype(F32).astype(BF16)
    requarter = (col == ((row % 16) // 4) * 16 + (row // 16) * 4 + row % 4).astype(F32).astype(BF16)

    for load in loads[:5]:
        load.wait()
    for at, value in ((64, group_taps_v[...]), (68, group_bias_v[...])):
        high = value.astype(BF16).astype(F32)
        packed_taps[pl.ds(at, value.shape[0]), :] = high
        packed_taps[pl.ds(at + 8, value.shape[0]), :] = value - high
    maps_partial = mm_nt(w_group[...], tokens[...]).astype(BF16)
    regrouped = mm(regroup, maps_partial)
    tail = regrouped[:, PROMPT:] + mm_nt(regroup, packed_taps[...].astype(BF16))
    a_src[:, :, pl.ds(0, PROMPT)] = regrouped[:, :PROMPT].reshape(8, 8, PROMPT).astype(BF16)
    a_src[:, :, pl.ds(PROMPT, 128)] = tail.reshape(8, 8, 128).astype(BF16)

    pl.semaphore_wait(
        barrier, 19 + jnp.where(quarter != low, 1, 0) + jnp.where(samp != low, 1, 0)
    )

    def a_copy(g):
        return copy(a_src.at[g], a_dst.at[place], a_send.at[g], a_recv.at[place], samp, g * 4 + low)

    for g in range(8):
        @pl.when(g * 4 + low != tp)
        def _():
            a_copy(g).start()

        @pl.when(g * 4 + low == tp)
        def _():
            a_dst[pl.ds(place, 1)] = a_src[pl.ds(g, 1)]

    lane_h = iota((160, 128), 1)

    def packed(part, h):
        upper = part[:160, 128 * (h // 2):128 * (h // 2) + 128]
        lower = part[160:, 128 * (h // 2):128 * (h // 2) + 128]
        if h % 2 == 0:
            return jnp.where(lane_h < 64, upper, pltpu.roll(lower, 64, 1)).astype(BF16)
        return jnp.where(lane_h < 64, pltpu.roll(upper, 64, 1), lower).astype(BF16)

    def to_heads(source, target, send, recv):
        return [
            copy(source.at[(samp + d) % 4], target.at[d - 1], send.at[d - 1], recv.at[d - 1], (samp + d) % 4, tp)
            for d in (2, 1, 3)
        ]

    loads[5].wait()
    sizes = mm_nt(w_step[...], tokens[...])
    loads[6].wait()
    head_part = mm(tokens[pl.ds(0, ROWS), :], w_in[1])
    size_row = iota((16, 128), 0)
    for h in range(4):
        x_src[h, pl.ds(0, 160), :] = packed(head_part, h)
        piece = jnp.zeros((16, 128), F32)
        for b in range(3):
            piece = jnp.where(size_row == b, sizes[h:h + 1, 128 * b:128 * b + 128], piece)
        x_src[h, pl.ds(160, 16), :] = piece.astype(BF16)
    x_copies = start(to_heads(x_src, x_dst, x_send, x_recv))
    loads[7].wait()
    gate_part = mm(tokens[pl.ds(0, ROWS), :], w_in[0])
    for h in range(4):
        z_src[h] = packed(gate_part, h)

    for i in range(8):
        @pl.when(quarter * 8 + i != tp)
        def _():
            pltpu.make_async_copy(a_dst.at[i], a_dst.at[i], a_recv.at[i]).wait()
    own_maps = a_dst[...].astype(F32).reshape(64, PADDED)
    lane_q = iota((32, 128), 1)
    fresh_maps = own_maps[:, PROMPT:]
    b_src[pl.ds(0, 64), :] = own_maps[:, 0:128].astype(BF16)
    b_src[pl.ds(64, 64), :] = own_maps[:, 128:256].astype(BF16)
    b_src[pl.ds(128, 32), :] = jnp.where(lane_q < 64, fresh_maps[:32], pltpu.roll(fresh_maps[32:], 64, 1)).astype(BF16)
    b_copies = start([
        copy(b_src, b_dst.at[d - 1], b_send.at[d - 1], b_recv.at[d - 1], (samp + d) % 4, tp) for d in (2, 1, 3)
    ])

    for load in loads[13:]:
        load.wait()
    gain = jnp.transpose(jnp.broadcast_to(gain_v[...], (128, CHANNELS)))
    for to in range(4):
        for part in range(4):
            columns = pl.ds(512 * to + 128 * part, 128)
            w_src[to, :, pl.ds(128 * part, 128)] = (w_out[:, columns].astype(F32) * gain).astype(BF16)
    w_all[pl.ds(across, 1)] = w_src[pl.ds(across, 1)]
    w_copies = start([
        copy(
            w_src.at[(across + d) % 4], w_all.at[across], w_send.at[d - 1], w_recv.at[d - 1],
            samp, low * 8 + ((across + d) % 4) * 2 + core,
        )
        for d in (2, 1, 3)
    ])

    lane128 = iota((1, 128), 1)

    def of_head(value):
        chosen = jnp.zeros((value.shape[0], 128), F32)
        for h in range(4):
            half = value[:, 128 * (h // 2):128 * (h // 2) + 128]
            if h % 2 == 0:
                half = pltpu.roll(half, 64, 1)
            chosen = jnp.where(samp == h, half, chosen)
        return jnp.where(lane128 >= 64, chosen, 0.0)

    def own_scalar(ref):
        return jnp.sum(jnp.where(iota((1, 4), 1) == samp, ref[...], 0.0), axis=1, keepdims=True)

    def unpacked(value):
        return jnp.concatenate([pltpu.roll(value, 64, 1), value], axis=0)

    for load in loads[8:13]:
        load.wait()
    taps8 = of_head(jnp.concatenate([taps_v[...], bias_v[...], jnp.zeros((3, CHANNELS), F32)], axis=0))
    skip = own_scalar(skip_v)
    step_bias = own_scalar(step_bias_v)
    rate = jnp.exp(own_scalar(decay_v))
    for one in x_copies:
        one.wait_recv()
    z_copies = start(to_heads(z_src, z_dst, z_send, z_recv))
    summed = x_src[samp].astype(F32)
    for d in range(3):
        summed = summed + x_dst[d].astype(F32)
    summed = summed.astype(BF16).astype(F32)
    heads = unpacked(summed[:160])
    before = heads[:PROMPT]
    row_p = iota((PROMPT, 128), 0)
    conv = taps8[4:5] + taps8[3:4] * before
    for k in range(1, 4):
        conv = conv + taps8[3 - k:4 - k] * jnp.where(row_p >= k, pltpu.roll(before, k, 0), 0.0)
    mixed[pl.ds(0, PROMPT), :] = silu(conv).astype(BF16)
    line = jnp.concatenate(
        [jnp.broadcast_to(before[253 + k:254 + k], (16, 128)) for k in range(3)] + [heads[PROMPT:ROWS]], axis=0
    )
    conv = taps8[4:5] + taps8[0:1] * line[0:64]
    for k in range(1, 4):
        conv = conv + taps8[k:k + 1] * line[16 * k:16 * k + 64]
    mixed[pl.ds(PROMPT, FRESH), :] = silu(conv).astype(BF16)

    size = jnp.concatenate([summed[160 + b:161 + b] for b in range(3)], axis=1)
    size = jnp.broadcast_to(size, (8, PADDED)) + step_bias
    size = jnp.maximum(size, 0.0) + jnp.log1p(jnp.exp(-jnp.abs(size)))
    logs = -size * rate
    run = logs[:, :PROMPT]
    lane_r = iota((8, PROMPT), 1)
    for k in (1, 2, 4, 8, 16, 32, 64, 128):
        run = run + jnp.where(lane_r >= k, pltpu.roll(run, k, 1), 0.0)
    run_f = logs[:, PROMPT:]
    lane_s = iota((8, 128), 1)
    for k in (16, 32):
        run_f = run_f + jnp.where(lane_s >= k, pltpu.roll(run_f, k, 1), 0.0)
    run_f = run_f + run[:, PROMPT - 1:PROMPT]
    runs = [run[0:1, 0:128], run[0:1, 128:256], run_f[0:1]]
    trail = jnp.concatenate([jnp.transpose(jnp.broadcast_to(r, (128, 128))) for r in runs], axis=0)[:ROWS]
    lane = iota((128, 128), 1)
    row_q = iota((128, 128), 0)
    tiles = ((256, 64, 0), (256, 64, 1), (256, 64, 2), (0, 128, 0), (128, 128, 0), (128, 128, 1))
    offsets = (0, 64, 128, 192, 320, 448)
    for (first, count, b), offset in zip(tiles, offsets):
        gap = trail[first:first + count] - runs[b]
        if b == 2:
            seen = jnp.logical_and(lane <= row_q, lane % 16 == row_q % 16)[:count]
            gap = jnp.where(seen, gap, -1e30)
        elif first == 128 * b:
            gap = jnp.where(lane <= row_q, gap, -1e30)
        weights[pl.ds(offset, count), :] = jnp.exp(gap) * size[0:1, 128 * b:128 * b + 128]

    for one in b_copies:
        one.wait_recv()
    total = b_src[...].astype(F32)
    for d in range(3):
        total = total + b_dst[d].astype(F32)
    total = total.astype(BF16).astype(F32)
    taps = [own_maps[:, 320 + k:321 + k] + own_maps[:, 328 + k:329 + k] for k in range(5)]
    before = jnp.concatenate([total[0:64], total[64:128]], axis=1)
    lane_p = iota((64, PROMPT), 1)
    conv = taps[4] + taps[3] * before
    for k in range(1, 4):
        conv = conv + taps[3 - k] * jnp.where(lane_p >= k, pltpu.roll(before, k, 1), 0.0)
    maps_prompt = silu(conv).astype(BF16)
    lane_f = iota((64, 128), 1)
    line = jnp.concatenate([total[128:160], pltpu.roll(total[128:160], 64, 1)], axis=0)
    line = pltpu.roll(line, 48, 1)
    for k in range(3):
        line = jnp.where(
            jnp.logical_and(lane_f >= 16 * k, lane_f < 16 * k + 16), before[:, 253 + k:254 + k], line
        )
    conv = taps[4] + taps[0] * line
    for k in range(1, 4):
        conv = conv + taps[k] * pltpu.roll(line, 128 - 16 * k, 1)
    maps_fresh = jnp.where(lane_f < 64, silu(conv), 0.0).astype(BF16)
    maps[quarter, :, pl.ds(0, PROMPT)] = maps_prompt
    maps[quarter, :, pl.ds(PROMPT, 128)] = maps_fresh
    c_copies = start([
        copy(maps.at[quarter], maps.at[quarter], c_send.at[d - 1], c_recv.at[d - 1], samp, group * 4 + (quarter + d) % 4)
        for d in (3, 2, 1)
    ])
    for one in c_copies:
        one.wait_recv()
    inputs = jnp.concatenate([maps[0], maps[1]], axis=0)
    to_read = jnp.concatenate([maps[2], maps[3]], axis=0).astype(F32)
    readout = jnp.transpose(to_read).astype(BF16)

    def read(first, count, blocks):
        value = skip * mixed[pl.ds(first, count), :].astype(F32)
        for b, offset in blocks:
            products = mm(readout[first:first + count], inputs[:, 128 * b:128 * b + 128])
            seen = (weights[pl.ds(offset, count), :] * products).astype(BF16)
            value = value + mm(seen, mixed[pl.ds(128 * b, 128), :])
        return value

    fresh = read(256, 64, ((0, 0), (1, 64), (2, 128)))
    halves = [read(0, 128, ((0, 192),)), read(128, 128, ((0, 320), (1, 448)))]
    for one in z_copies:
        one.wait_recv()
    gate = z_src[samp].astype(F32)
    for d in range(3):
        gate = gate + z_dst[d].astype(F32)
    gate = silu(unpacked(gate.astype(BF16).astype(F32)))
    fresh = mm(requarter, (fresh * gate[PROMPT:]).astype(BF16))

    lane_c = iota((BLOCK, 128), 1)
    g_copies = []

    def onward(c, k):
        piece = (samp - k + 4) % 4
        return [
            copy(
                gat.at[c, across, piece], gat.at[c, across, piece], f_send.at[c, k, d - 1], f_recv.at[c, k, d - 1],
                samp, low * 8 + ((across + d) % 4) * 2 + core,
            )
            for d in (2, 1, 3)
        ]

    f_copies = [[], []]
    for c in range(2):
        gated = halves[c] * gate[128 * c:128 * c + 128]
        upper = jnp.concatenate([gated[:64], fresh[32 * c:32 * c + 16]], axis=0)
        lower = jnp.concatenate([gated[64:], fresh[32 * c + 16:32 * c + 32]], axis=0)
        gat[c, across, samp] = jnp.where(lane_c < 64, pltpu.roll(upper, 64, 1), lower).astype(BF16)
        g_copies.append(start([
            copy(
                gat.at[c, across, samp], gat.at[c, across, samp], g_send.at[c, d - 1], g_recv.at[c, d - 1],
                (samp + d) % 4, tp,
            )
            for d in (2, 1, 3)
        ]))
        f_copies[c] += start(onward(c, 0))
    for c in range(2):
        for k, at in ((1, 1), (3, 2), (2, 0)):
            g_copies[c][at].wait_recv()
            f_copies[c] += start(onward(c, k))

    partner = low * 8 + across * 2 + 1 - core
    sq_lane = iota((2 * BLOCK, 128), 1)
    for one in w_copies:
        one.wait_recv()
    e_copies = []
    for c in range(2):
        for one in f_copies[c]:
            one.wait_recv()
        squares = []
        for half in range(2):
            total = jnp.zeros((2 * BLOCK, 128), F32)
            for at in (2 * half, 2 * half + 1):
                for pair in range(2):
                    first, second = gat[c, at, 2 * pair].astype(F32), gat[c, at, 2 * pair + 1].astype(F32)
                    both = jnp.concatenate([
                        jnp.where(lane_c < 64, first, pltpu.roll(second, 64, 1)),
                        jnp.where(lane_c < 64, pltpu.roll(first, 64, 1), second),
                    ], axis=0)
                    gathered[:, pl.ds(256 * at + 128 * pair, 128)] = both.astype(BF16)
                    total = total + both * both
            squares.append(jnp.sum(total, axis=1, keepdims=True))
        sq_src[c] = jnp.where(sq_lane < 64, squares[0], squares[1])
        q_copies = start([copy(sq_src.at[c], sq_dst.at[c], q_send.at[c], q_recv.at[c], samp, partner)])
        products = [
            mm(gathered[:, pl.ds(512 * half, 512)], w_all[2 * half:2 * half + 2].reshape(512, 512)) for half in range(2)
        ]
        q_copies[0].wait_recv()
        scale = lax.rsqrt((sq_src[c] + sq_dst[c]) * (1.0 / 1024.0) + 1e-5)
        scaled = products[0] * scale[:, 0:1] + products[1] * scale[:, 64:65]
        product[c, 0] = scaled[:, :256]
        product[c, 1] = scaled[:, 256:]
        e_src[c] = product[c, 1 - core].astype(BF16)
        e_copies += start([copy(e_src.at[c], e_dst.at[c], e_send.at[c], e_recv.at[c], samp, partner)])

    def d3_copy(s):
        return copy(d3_src.at[s], d3_dst.at[low], d3_send.at[s], d3_recv.at[low], s, samp * 8 + place)

    def stays(s):
        return jnp.logical_and(samp == low, samp == s)

    for c in range(2):
        e_copies[c].wait_recv()
        outer = jnp.logical_or(samp == 0, samp == 3)
        far = jnp.where(outer, 1 - c, c)
        for half in (far, 1 - far):
            rows = pl.ds(pl.multiple_of(BLOCK * half, 16), BLOCK)
            s = 2 * c + half
            d3_src[s] = (product[c, core, rows, :] + e_dst[c, rows, :].astype(F32)).astype(BF16)

            @pl.when(stays(s))
            def _():
                d3_dst[low] = d3_src[s]

            @pl.when(jnp.logical_not(stays(s)))
            def _():
                d3_copy(s).start()

    for i in range(4):
        @pl.when(jnp.logical_or(low != samp, i != low))
        def _():
            pltpu.make_async_copy(d3_dst.at[i], d3_dst.at[i], d3_recv.at[i]).wait()
    value = d3_dst[0].astype(F32)
    for i in range(1, 4):
        value = value + d3_dst[i].astype(F32)
    prefill_ref[...] = value[:64]
    for step in range(4):
        decode_ref[step] = value[64 + 4 * step:68 + 4 * step]

    for g in range(8):
        @pl.when(g * 4 + low != tp)
        def _():
            a_copy(g).wait_send()
    for one in sends:
        one.wait_send()
    for s in range(4):
        @pl.when(jnp.logical_not(stays(s)))
        def _():
            d3_copy(s).wait_send()


def shards(
    prompt_tokens, step_tokens, lengths, input_weight, group_weight, step_weight,
    conv_weight, group_conv, conv_bias, group_bias, step_bias, decay_log, skip_gain, norm_gain, output_weight,
):
    anywhere = pl.BlockSpec(memory_space=pl.ANY)
    vector = pl.BlockSpec(memory_space=pltpu.VMEM)

    def dma(*shape):
        return pltpu.SemaphoreType.DMA(shape)

    def room(*shape):
        return pltpu.VMEM(shape, BF16)

    def wide_room(*shape):
        return pltpu.VMEM(shape, F32)

    prefill, decode = pl.pallas_call(
        kernel,
        out_shape=(
            jax.ShapeDtypeStruct((64, CHANNELS), F32),
            jax.ShapeDtypeStruct((4, 4, CHANNELS), F32),
        ),
        in_specs=[anywhere] * 14,
        out_specs=(vector, vector),
        scratch_shapes=[
            room(PADDED, WIDTH), room(2, WIDTH, CHANNELS), room(64, WIDTH), room(CHANNELS, WIDTH), room(4, WIDTH),
            wide_room(4, CHANNELS), wide_room(1, CHANNELS), wide_room(4, 64), wide_room(1, 64),
            wide_room(1, 4), wide_room(1, 4), wide_room(1, 4), wide_room(1, CHANNELS), dma(15),
            wide_room(128, 64),
            room(8, 8, PADDED), room(8, 8, PADDED),
            room(160, 128), room(3, 160, 128),
            room(4, 64, PADDED),
            room(4, 176, 128), room(3, 176, 128),
            room(4, 160, 128), room(3, 160, 128),
            room(4, CHANNELS, 512), room(4, CHANNELS, 512),
            room(PADDED, 128), wide_room(576, 128),
            room(2, 4, 4, BLOCK, 128), room(2 * BLOCK, 1024),
            wide_room(2, 2 * BLOCK, 128), wide_room(2, 2 * BLOCK, 128),
            wide_room(2, 2, 2 * BLOCK, CHANNELS), room(2, 2 * BLOCK, CHANNELS), room(2, 2 * BLOCK, CHANNELS),
            room(4, BLOCK, CHANNELS), room(4, BLOCK, CHANNELS),
            dma(8), dma(8), dma(3), dma(3), dma(3), dma(3), dma(3), dma(3), dma(3), dma(3), dma(3), dma(3),
            dma(2, 3), dma(2, 3), dma(2, 4, 3), dma(2, 4, 3), dma(2), dma(2), dma(2), dma(2), dma(4), dma(4),
        ],
        compiler_params=pltpu.CompilerParams(
            collective_id=0, has_side_effects=True, vmem_limit_bytes=VMEM_LIMIT
        ),
        cost_estimate=pl.CostEstimate(flops=2 * 10**9, bytes_accessed=8 * 10**6, transcendentals=10**6),
    )(
        prompt_tokens.reshape(PROMPT, WIDTH),
        step_tokens.reshape(FRESH, WIDTH),
        input_weight,
        group_weight.T,
        output_weight,
        step_weight.T,
        conv_weight,
        conv_bias.reshape(1, CHANNELS),
        group_conv,
        group_bias.reshape(1, 64),
        step_bias.reshape(1, 4),
        decay_log.reshape(1, 4),
        skip_gain.reshape(1, 4),
        norm_gain.reshape(1, CHANNELS),
    )
    active = jnp.arange(4)[:, None, None] < lengths[None]
    decode = jnp.where(active, decode, 0.0).astype(BF16)
    return prefill.astype(BF16)[:, None, :], decode[:, :, None, :]


def solution(mesh):
    placed = (
        P(None, "rep", "samp"),
        P(None, None, "rep", "samp"),
        P("samp", "rep"),
        P(None, "samp", "tp"),
        P("samp", "tp"),
        P("samp", "tp"),
        P(None, "tp"),
        P(None, "tp"),
        P("tp"),
        P("tp"),
        P("tp"),
        P("tp"),
        P("tp"),
        P("tp"),
        P("tp", "samp"),
    )
    return jax.shard_map(
        shards,
        mesh=mesh,
        in_specs=placed,
        out_specs=(P("samp", "rep", "tp"), P(None, "samp", "rep", "tp")),
        check_vma=False,
    )
```

```python
import jax
import jax.numpy as jnp
from jax import lax
from jax.experimental import pallas as pl
from jax.experimental.pallas import tpu as pltpu
from jax.sharding import PartitionSpec as P

PROMPT = 256
FRESH = 64
ROWS = 320
PADDED = 384
WIDTH = 2048
CHANNELS = 256
BLOCK = 80
VMEM_LIMIT = 60 * 1024 * 1024
MESH = pl.DeviceIdType.MESH
F32 = jnp.float32
BF16 = jnp.bfloat16
NT = (((1,), (1,)), ((), ()))


def mm(a, b):
    return jnp.dot(a, b, preferred_element_type=F32)


def mm_nt(a, b):
    return lax.dot_general(a, b, NT, preferred_element_type=F32)


def iota(shape, axis):
    return lax.broadcasted_iota(jnp.int32, shape, axis)


def silu(v):
    return v / (1.0 + jnp.exp(-v))


def kernel(
    prompt_ref, fresh_ref, in_ref, group_ref, out_ref, step_ref, taps_ref, bias_ref,
    group_taps_ref, group_bias_ref, step_bias_ref, decay_ref, skip_ref, gain_ref,
    rows_ref,
    tokens, w_in, w_group, w_out, w_step, taps_v, bias_v, group_taps_v, group_bias_v,
    step_bias_v, decay_v, skip_v, gain_v, load_sem,
    packed_taps, a_src, a_dst, b_src, b_dst, maps, x_src, x_dst, z_src, z_dst,
    w_src, w_all, mixed, weights, gat, gathered, sq_all,
    product, e_src, e_dst, d3_src, d3_dst,
    a_send, a_recv, b_send, b_recv, c_send, c_recv, x_send, x_recv, z_send, z_recv, w_send, w_recv,
    g_send, g_recv, f_send, f_recv, q_send, q_recv, e_send, e_recv, d3_send, d3_recv,
):
    rep = lax.axis_index("rep")
    samp = lax.axis_index("samp")
    tp = lax.axis_index("tp")
    low = tp // 8
    place = tp % 8
    across = place // 2
    core = place % 2
    group = tp // 4
    quarter = tp % 4

    def device(samp_index, tp_index):
        return (rep, samp_index, tp_index)

    pairs = (
        (group_ref, w_group), (prompt_ref, tokens.at[pl.ds(0, PROMPT)]), (fresh_ref, tokens.at[pl.ds(PROMPT, FRESH)]),
        (group_taps_ref, group_taps_v), (group_bias_ref, group_bias_v), (step_ref, w_step),
        (in_ref.at[1], w_in.at[1]), (in_ref.at[0], w_in.at[0]), (taps_ref, taps_v), (bias_ref, bias_v),
        (step_bias_ref, step_bias_v), (decay_ref, decay_v), (skip_ref, skip_v), (gain_ref, gain_v), (out_ref, w_out),
    )
    loads = [pltpu.make_async_copy(a, b, load_sem.at[i]) for i, (a, b) in enumerate(pairs)]
    for load in loads[:3]:
        load.start()

    barrier = pltpu.get_barrier_semaphore()

    def greet(samp_index, tp_index):
        pl.semaphore_signal(barrier, inc=1, device_id=device(samp_index, tp_index), device_id_type=MESH)

    for d in (2, 1, 3):
        greet((samp + d) % 4, tp)
    for i in range(4):
        @pl.when(jnp.logical_or(low != samp, i != low))
        def _():
            greet(low, i * 8 + place)
    for i in range(8):
        @pl.when(quarter * 8 + i != tp)
        def _():
            greet(samp, quarter * 8 + i)
    for d in range(1, 4):
        greet(samp, group * 4 + (quarter + d) % 4)
        greet(samp, low * 8 + ((across + d) % 4) * 2 + core)
        greet(samp, low * 8 + ((across + d) % 4) * 2 + 1 - core)

    for load in loads[3:]:
        load.start()
    sends = []

    def copy(source, target, send, recv, samp_index, tp_index):
        return pltpu.make_async_remote_copy(
            src_ref=source, dst_ref=target, send_sem=send, recv_sem=recv,
            device_id=device(samp_index, tp_index), device_id_type=MESH,
        )

    def start(copies):
        for one in copies:
            one.start()
            sends.append(one)
        return copies

    tokens[pl.ds(ROWS, PADDED - ROWS), :] = jnp.zeros((PADDED - ROWS, WIDTH), BF16)
    packed_taps[...] = jnp.zeros(packed_taps.shape, F32)
    mixed[pl.ds(ROWS, PADDED - ROWS), :] = jnp.zeros((PADDED - ROWS, 128), BF16)

    row = iota((64, 64), 0)
    col = iota((64, 64), 1)
    regroup = (col == (row % 8) * 8 + row // 8).astype(F32).astype(BF16)
    requarter = (col == ((row % 16) // 4) * 16 + (row // 16) * 4 + row % 4).astype(F32).astype(BF16)

    for load in loads[:5]:
        load.wait()
    for at, value in ((64, group_taps_v[...]), (68, group_bias_v[...])):
        high = value.astype(BF16).astype(F32)
        packed_taps[pl.ds(at, value.shape[0]), :] = high
        packed_taps[pl.ds(at + 8, value.shape[0]), :] = value - high
    maps_partial = mm_nt(w_group[...], tokens[...]).astype(BF16)
    regrouped = mm(regroup, maps_partial)
    tail = regrouped[:, PROMPT:] + mm_nt(regroup, packed_taps[...].astype(BF16))
    a_src[:, :, pl.ds(0, PROMPT)] = regrouped[:, :PROMPT].reshape(8, 8, PROMPT).astype(BF16)
    a_src[:, :, pl.ds(PROMPT, 128)] = tail.reshape(8, 8, 128).astype(BF16)

    pl.semaphore_wait(
        barrier, 22 + jnp.where(quarter != low, 1, 0) + jnp.where(samp != low, 1, 0)
    )

    def a_copy(g):
        return copy(a_src.at[g], a_dst.at[place], a_send.at[g], a_recv.at[place], samp, g * 4 + low)

    for g in range(8):
        @pl.when(g * 4 + low != tp)
        def _():
            a_copy(g).start()

        @pl.when(g * 4 + low == tp)
        def _():
            a_dst[pl.ds(place, 1)] = a_src[pl.ds(g, 1)]

    lane_h = iota((160, 128), 1)

    def packed(part, h):
        upper = part[:160, 128 * (h // 2):128 * (h // 2) + 128]
        lower = part[160:, 128 * (h // 2):128 * (h // 2) + 128]
        if h % 2 == 0:
            return jnp.where(lane_h < 64, upper, pltpu.roll(lower, 64, 1)).astype(BF16)
        return jnp.where(lane_h < 64, pltpu.roll(upper, 64, 1), lower).astype(BF16)

    def to_heads(source, target, send, recv):
        return [
            copy(source.at[(samp + d) % 4], target.at[d - 1], send.at[d - 1], recv.at[d - 1], (samp + d) % 4, tp)
            for d in (2, 1, 3)
        ]

    loads[5].wait()
    sizes = mm_nt(w_step[...], tokens[...])
    loads[6].wait()
    head_part = mm(tokens[pl.ds(0, ROWS), :], w_in[1])
    size_row = iota((16, 128), 0)
    for h in range(4):
        x_src[h, pl.ds(0, 160), :] = packed(head_part, h)
        piece = jnp.zeros((16, 128), F32)
        for b in range(3):
            piece = jnp.where(size_row == b, sizes[h:h + 1, 128 * b:128 * b + 128], piece)
        x_src[h, pl.ds(160, 16), :] = piece.astype(BF16)
    x_copies = start(to_heads(x_src, x_dst, x_send, x_recv))
    loads[7].wait()
    gate_part = mm(tokens[pl.ds(0, ROWS), :], w_in[0])
    for h in range(4):
        z_src[h] = packed(gate_part, h)

    for i in range(8):
        @pl.when(quarter * 8 + i != tp)
        def _():
            pltpu.make_async_copy(a_dst.at[i], a_dst.at[i], a_recv.at[i]).wait()
    own_maps = a_dst[...].astype(F32).reshape(64, PADDED)
    lane_q = iota((32, 128), 1)
    fresh_maps = own_maps[:, PROMPT:]
    b_src[pl.ds(0, 64), :] = own_maps[:, 0:128].astype(BF16)
    b_src[pl.ds(64, 64), :] = own_maps[:, 128:256].astype(BF16)
    b_src[pl.ds(128, 32), :] = jnp.where(lane_q < 64, fresh_maps[:32], pltpu.roll(fresh_maps[32:], 64, 1)).astype(BF16)
    b_copies = start([
        copy(b_src, b_dst.at[d - 1], b_send.at[d - 1], b_recv.at[d - 1], (samp + d) % 4, tp) for d in (2, 1, 3)
    ])

    for load in loads[13:]:
        load.wait()
    gain = jnp.transpose(jnp.broadcast_to(gain_v[...], (128, CHANNELS)))
    for to in range(4):
        for part in range(4):
            columns = pl.ds(512 * to + 128 * part, 128)
            w_src[to, :, pl.ds(128 * part, 128)] = (w_out[:, columns].astype(F32) * gain).astype(BF16)
    w_all[pl.ds(across, 1)] = w_src[pl.ds(across, 1)]
    w_copies = start([
        copy(
            w_src.at[(across + d) % 4], w_all.at[across], w_send.at[d - 1], w_recv.at[d - 1],
            samp, low * 8 + ((across + d) % 4) * 2 + core,
        )
        for d in (2, 1, 3)
    ])

    lane128 = iota((1, 128), 1)

    def of_head(value):
        chosen = jnp.zeros((value.shape[0], 128), F32)
        for h in range(4):
            half = value[:, 128 * (h // 2):128 * (h // 2) + 128]
            if h % 2 == 0:
                half = pltpu.roll(half, 64, 1)
            chosen = jnp.where(samp == h, half, chosen)
        return jnp.where(lane128 >= 64, chosen, 0.0)

    def own_scalar(ref):
        return jnp.sum(jnp.where(iota((1, 4), 1) == samp, ref[...], 0.0), axis=1, keepdims=True)

    def unpacked(value):
        return jnp.concatenate([pltpu.roll(value, 64, 1), value], axis=0)

    for load in loads[8:13]:
        load.wait()
    taps8 = of_head(jnp.concatenate([taps_v[...], bias_v[...], jnp.zeros((3, CHANNELS), F32)], axis=0))
    skip = own_scalar(skip_v)
    step_bias = own_scalar(step_bias_v)
    rate = jnp.exp(own_scalar(decay_v))
    for one in x_copies:
        one.wait_recv()
    z_copies = start(to_heads(z_src, z_dst, z_send, z_recv))
    summed = x_src[samp].astype(F32)
    for d in range(3):
        summed = summed + x_dst[d].astype(F32)
    summed = summed.astype(BF16).astype(F32)
    heads = unpacked(summed[:160])
    before = heads[:PROMPT]
    row_p = iota((PROMPT, 128), 0)
    conv = taps8[4:5] + taps8[3:4] * before
    for k in range(1, 4):
        conv = conv + taps8[3 - k:4 - k] * jnp.where(row_p >= k, pltpu.roll(before, k, 0), 0.0)
    mixed[pl.ds(0, PROMPT), :] = silu(conv).astype(BF16)
    line = jnp.concatenate(
        [jnp.broadcast_to(before[253 + k:254 + k], (16, 128)) for k in range(3)] + [heads[PROMPT:ROWS]], axis=0
    )
    conv = taps8[4:5] + taps8[0:1] * line[0:64]
    for k in range(1, 4):
        conv = conv + taps8[k:k + 1] * line[16 * k:16 * k + 64]
    mixed[pl.ds(PROMPT, FRESH), :] = silu(conv).astype(BF16)

    size = jnp.concatenate([summed[160 + b:161 + b] for b in range(3)], axis=1)
    size = jnp.broadcast_to(size, (8, PADDED)) + step_bias
    size = jnp.maximum(size, 0.0) + jnp.log1p(jnp.exp(-jnp.abs(size)))
    logs = -size * rate
    run = logs[:, :PROMPT]
    lane_r = iota((8, PROMPT), 1)
    for k in (1, 2, 4, 8, 16, 32, 64, 128):
        run = run + jnp.where(lane_r >= k, pltpu.roll(run, k, 1), 0.0)
    run_f = logs[:, PROMPT:]
    lane_s = iota((8, 128), 1)
    for k in (16, 32):
        run_f = run_f + jnp.where(lane_s >= k, pltpu.roll(run_f, k, 1), 0.0)
    run_f = run_f + run[:, PROMPT - 1:PROMPT]
    runs = [run[0:1, 0:128], run[0:1, 128:256], run_f[0:1]]
    trail = jnp.concatenate([jnp.transpose(jnp.broadcast_to(r, (128, 128))) for r in runs], axis=0)[:ROWS]
    lane = iota((128, 128), 1)
    row_q = iota((128, 128), 0)
    tiles = ((256, 64, 0), (256, 64, 1), (256, 64, 2), (0, 128, 0), (128, 128, 0), (128, 128, 1))
    offsets = (0, 64, 128, 192, 320, 448)
    for (first, count, b), offset in zip(tiles, offsets):
        gap = trail[first:first + count] - runs[b]
        if b == 2:
            seen = jnp.logical_and(lane <= row_q, lane % 16 == row_q % 16)[:count]
            gap = jnp.where(seen, gap, -1e30)
        elif first == 128 * b:
            gap = jnp.where(lane <= row_q, gap, -1e30)
        weights[pl.ds(offset, count), :] = jnp.exp(gap) * size[0:1, 128 * b:128 * b + 128]

    for one in b_copies:
        one.wait_recv()
    total = b_src[...].astype(F32)
    for d in range(3):
        total = total + b_dst[d].astype(F32)
    total = total.astype(BF16).astype(F32)
    taps = [own_maps[:, 320 + k:321 + k] + own_maps[:, 328 + k:329 + k] for k in range(5)]
    before = jnp.concatenate([total[0:64], total[64:128]], axis=1)
    lane_p = iota((64, PROMPT), 1)
    conv = taps[4] + taps[3] * before
    for k in range(1, 4):
        conv = conv + taps[3 - k] * jnp.where(lane_p >= k, pltpu.roll(before, k, 1), 0.0)
    maps_prompt = silu(conv).astype(BF16)
    lane_f = iota((64, 128), 1)
    line = jnp.concatenate([total[128:160], pltpu.roll(total[128:160], 64, 1)], axis=0)
    line = pltpu.roll(line, 48, 1)
    for k in range(3):
        line = jnp.where(
            jnp.logical_and(lane_f >= 16 * k, lane_f < 16 * k + 16), before[:, 253 + k:254 + k], line
        )
    conv = taps[4] + taps[0] * line
    for k in range(1, 4):
        conv = conv + taps[k] * pltpu.roll(line, 128 - 16 * k, 1)
    maps_fresh = jnp.where(lane_f < 64, silu(conv), 0.0).astype(BF16)
    maps[quarter, :, pl.ds(0, PROMPT)] = maps_prompt
    maps[quarter, :, pl.ds(PROMPT, 128)] = maps_fresh
    c_copies = start([
        copy(maps.at[quarter], maps.at[quarter], c_send.at[d - 1], c_recv.at[d - 1], samp, group * 4 + (quarter + d) % 4)
        for d in (3, 2, 1)
    ])
    for one in c_copies:
        one.wait_recv()
    inputs = jnp.concatenate([maps[0], maps[1]], axis=0)
    to_read = jnp.concatenate([maps[2], maps[3]], axis=0).astype(F32)
    readout = jnp.transpose(to_read).astype(BF16)

    def read(first, count, blocks):
        value = skip * mixed[pl.ds(first, count), :].astype(F32)
        for b, offset in blocks:
            products = mm(readout[first:first + count], inputs[:, 128 * b:128 * b + 128])
            seen = (weights[pl.ds(offset, count), :] * products).astype(BF16)
            value = value + mm(seen, mixed[pl.ds(128 * b, 128), :])
        return value

    fresh = read(256, 64, ((0, 0), (1, 64), (2, 128)))
    halves = [read(0, 128, ((0, 192),)), read(128, 128, ((0, 320), (1, 448)))]
    for one in z_copies:
        one.wait_recv()
    gate = z_src[samp].astype(F32)
    for d in range(3):
        gate = gate + z_dst[d].astype(F32)
    gate = silu(unpacked(gate.astype(BF16).astype(F32)))
    fresh = mm(requarter, (fresh * gate[PROMPT:]).astype(BF16))

    blocks = []
    for i in range(4):
        half = halves[i // 2] * gate[128 * (i // 2):128 * (i // 2) + 128]
        blocks += [half[64 * (i % 2):64 * (i % 2) + 64], fresh[16 * i:16 * i + 16]]
    upper = jnp.concatenate(blocks[:4], axis=0)
    lower = jnp.concatenate(blocks[4:], axis=0)
    gat[across, samp] = jnp.where(lane_h < 64, pltpu.roll(upper, 64, 1), lower).astype(BF16)
    g_copies = start([
        copy(gat.at[across, samp], gat.at[across, samp], g_send.at[d - 1], g_recv.at[d - 1], (samp + d) % 4, tp)
        for d in (2, 1, 3)
    ])

    def onward(k):
        piece = (samp - k + 4) % 4
        return start([
            copy(
                gat.at[across, piece], gat.at[across, piece], f_send.at[k, d - 1], f_recv.at[k, d - 1],
                samp, low * 8 + ((across + d) % 4) * 2 + core,
            )
            for d in (2, 1, 3)
        ])

    f_copies = onward(0)
    for k, at in ((1, 1), (3, 2), (2, 0)):
        g_copies[at].wait_recv()
        f_copies += onward(k)

    def side_by_side(at, pair):
        first, second = gat[at, 2 * pair].astype(F32), gat[at, 2 * pair + 1].astype(F32)
        return jnp.concatenate([
            jnp.where(lane_h < 64, first, pltpu.roll(second, 64, 1)),
            jnp.where(lane_h < 64, pltpu.roll(first, 64, 1), second),
        ], axis=0)

    squares = [side_by_side(across, pair) for pair in range(2)]
    squares = jnp.sum(squares[0] * squares[0] + squares[1] * squares[1], axis=1, keepdims=True)
    squares = jnp.concatenate([squares, jnp.zeros((PADDED - ROWS, 1), F32)], axis=0)
    sq_all[place] = jnp.transpose(jnp.broadcast_to(squares, (PADDED, 128)))[0:1]

    def q_copy(i):
        return copy(sq_all.at[place], sq_all.at[place], q_send.at[i], q_recv.at[place], samp, low * 8 + i)

    for i in range(8):
        @pl.when(place != i)
        def _():
            q_copy(i).start()

    for one in w_copies + f_copies:
        one.wait_recv()
    for at in range(4):
        for pair in range(2):
            gathered[:, pl.ds(256 * at + 128 * pair, 128)] = side_by_side(at, pair).astype(BF16)
    products = [
        mm(gathered[:, pl.ds(512 * half, 512)], w_all[2 * half:2 * half + 2].reshape(512, 512)) for half in range(2)
    ]
    for i in range(8):
        @pl.when(place != i)
        def _():
            pltpu.make_async_copy(sq_all.at[i], sq_all.at[i], q_recv.at[i]).wait()
    scales = []
    for half in range(2):
        total = sq_all[4 * half] + sq_all[4 * half + 1] + sq_all[4 * half + 2] + sq_all[4 * half + 3]
        scale = jnp.broadcast_to(lax.rsqrt(total * (1.0 / 1024.0) + 1e-5), (128, PADDED))
        scale = jnp.transpose(scale)[:ROWS]
        scales.append(jnp.concatenate([scale] * 4, axis=1))
    scaled = products[0] * scales[0] + products[1] * scales[1]
    product[0] = scaled[:, :256]
    product[1] = scaled[:, 256:]
    e_src[...] = product[1 - core].astype(BF16)
    e_copy = start([copy(e_src, e_dst, e_send.at[0], e_recv.at[0], samp, low * 8 + across * 2 + 1 - core)])[0]

    def d3_copy(s):
        return copy(d3_src.at[s], d3_dst.at[low], d3_send.at[s], d3_recv.at[low], s, samp * 8 + place)

    def stays(s):
        return jnp.logical_and(samp == low, samp == s)

    e_copy.wait_recv()
    for d in (2, 1, 3, 0):
        s = (samp + d) % 4
        rows = pl.ds(pl.multiple_of(BLOCK * s, 16), BLOCK)
        d3_src[s] = (product[core, rows, :] + e_dst[rows, :].astype(F32)).astype(BF16)

        @pl.when(stays(s))
        def _():
            d3_dst[low] = d3_src[s]

        @pl.when(jnp.logical_not(stays(s)))
        def _():
            d3_copy(s).start()

    for i in range(4):
        @pl.when(jnp.logical_or(low != samp, i != low))
        def _():
            pltpu.make_async_copy(d3_dst.at[i], d3_dst.at[i], d3_recv.at[i]).wait()
    value = d3_dst[0].astype(F32)
    for i in range(1, 4):
        value = value + d3_dst[i].astype(F32)
    rows_ref[...] = value.astype(BF16)

    for i in range(8):
        @pl.when(place != i)
        def _():
            q_copy(i).wait_send()
    for g in range(8):
        @pl.when(g * 4 + low != tp)
        def _():
            a_copy(g).wait_send()
    for one in sends:
        one.wait_send()
    for s in range(4):
        @pl.when(jnp.logical_not(stays(s)))
        def _():
            d3_copy(s).wait_send()


def finish(rows_ref, lengths_ref, prefill_ref, decode_ref):
    prefill_ref[...] = rows_ref[:64]
    step = iota((16, CHANNELS), 0)
    lengths = jnp.zeros((16, CHANNELS), jnp.int32)
    for i in range(4):
        lengths = jnp.where(step % 4 == i, lengths_ref[0, i], lengths)
    decode = jnp.where(step // 4 < lengths, rows_ref[64:].astype(F32), 0.0).astype(BF16)
    for i in range(4):
        decode_ref[i] = decode[4 * i:4 * i + 4]


def shards(
    prompt_tokens, step_tokens, lengths, input_weight, group_weight, step_weight,
    conv_weight, group_conv, conv_bias, group_bias, step_bias, decay_log, skip_gain, norm_gain, output_weight,
):
    anywhere = pl.BlockSpec(memory_space=pl.ANY)
    vector = pl.BlockSpec(memory_space=pltpu.VMEM)

    def dma(*shape):
        return pltpu.SemaphoreType.DMA(shape)

    def room(*shape):
        return pltpu.VMEM(shape, BF16)

    def wide_room(*shape):
        return pltpu.VMEM(shape, F32)

    rows = pl.pallas_call(
        kernel,
        out_shape=jax.ShapeDtypeStruct((BLOCK, CHANNELS), BF16),
        in_specs=[anywhere] * 14,
        out_specs=vector,
        scratch_shapes=[
            room(PADDED, WIDTH), room(2, WIDTH, CHANNELS), room(64, WIDTH), room(CHANNELS, WIDTH), room(4, WIDTH),
            wide_room(4, CHANNELS), wide_room(1, CHANNELS), wide_room(4, 64), wide_room(1, 64),
            wide_room(1, 4), wide_room(1, 4), wide_room(1, 4), wide_room(1, CHANNELS), dma(15),
            wide_room(128, 64),
            room(8, 8, PADDED), room(8, 8, PADDED),
            room(160, 128), room(3, 160, 128),
            room(4, 64, PADDED),
            room(4, 176, 128), room(3, 176, 128),
            room(4, 160, 128), room(3, 160, 128),
            room(4, CHANNELS, 512), room(4, CHANNELS, 512),
            room(PADDED, 128), wide_room(576, 128),
            room(4, 4, 160, 128), room(ROWS, 1024), wide_room(8, 1, PADDED),
            wide_room(2, ROWS, CHANNELS), room(ROWS, CHANNELS), room(ROWS, CHANNELS),
            room(4, BLOCK, CHANNELS), room(4, BLOCK, CHANNELS),
            dma(8), dma(8), dma(3), dma(3), dma(3), dma(3), dma(3), dma(3), dma(3), dma(3), dma(3), dma(3),
            dma(3), dma(3), dma(4, 3), dma(4, 3), dma(8), dma(8), dma(1), dma(1), dma(4), dma(4),
        ],
        compiler_params=pltpu.CompilerParams(
            collective_id=0, has_side_effects=True, vmem_limit_bytes=VMEM_LIMIT
        ),
        cost_estimate=pl.CostEstimate(flops=2 * 10**9, bytes_accessed=8 * 10**6, transcendentals=10**6),
    )(
        prompt_tokens.reshape(PROMPT, WIDTH),
        step_tokens.reshape(FRESH, WIDTH),
        input_weight,
        group_weight.T,
        output_weight,
        step_weight.T,
        conv_weight,
        conv_bias.reshape(1, CHANNELS),
        group_conv,
        group_bias.reshape(1, 64),
        step_bias.reshape(1, 4),
        decay_log.reshape(1, 4),
        skip_gain.reshape(1, 4),
        norm_gain.reshape(1, CHANNELS),
    )
    prefill, decode = pl.pallas_call(
        finish,
        out_shape=(
            jax.ShapeDtypeStruct((64, CHANNELS), BF16),
            jax.ShapeDtypeStruct((4, 4, CHANNELS), BF16),
        ),
        in_specs=[vector, pl.BlockSpec(memory_space=pltpu.SMEM)],
        out_specs=(vector, vector),
    )(rows, lengths.reshape(1, 4))
    return prefill[:, None, :], decode[:, :, None, :]


def solution(mesh):
    placed = (
        P(None, "rep", "samp"),
        P(None, None, "rep", "samp"),
        P("samp", "rep"),
        P(None, "samp", "tp"),
        P("samp", "tp"),
        P("samp", "tp"),
        P(None, "tp"),
        P(None, "tp"),
        P("tp"),
        P("tp"),
        P("tp"),
        P("tp"),
        P("tp"),
        P("tp"),
        P("tp", "samp"),
    )
    return jax.shard_map(
        shards,
        mesh=mesh,
        in_specs=placed,
        out_specs=(P("samp", "rep", "tp"), P(None, "samp", "rep", "tp")),
        check_vma=False,
    )
```

```python
import jax
import jax.numpy as jnp
from jax import lax
from jax.experimental import pallas as pl
from jax.experimental.pallas import tpu as pltpu
from jax.sharding import PartitionSpec as P

PROMPT = 256
FRESH = 64
ROWS = 320
PADDED = 384
WIDTH = 2048
CHANNELS = 256
BLOCK = 80
VMEM_LIMIT = 60 * 1024 * 1024
MESH = pl.DeviceIdType.MESH
F32 = jnp.float32
BF16 = jnp.bfloat16
NT = (((1,), (1,)), ((), ()))


def mm(a, b):
    return jnp.dot(a, b, preferred_element_type=F32)


def mm_nt(a, b):
    return lax.dot_general(a, b, NT, preferred_element_type=F32)


def iota(shape, axis):
    return lax.broadcasted_iota(jnp.int32, shape, axis)


def silu(v):
    return v / (1.0 + jnp.exp(-v))


def kernel(
    prompt_ref, fresh_ref, in_ref, group_ref, out_ref, step_ref, taps_ref, bias_ref,
    group_taps_ref, group_bias_ref, step_bias_ref, decay_ref, skip_ref, gain_ref,
    rows_ref,
    tokens, w_in, w_group, w_out, w_step, taps_v, bias_v, group_taps_v, group_bias_v,
    step_bias_v, decay_v, skip_v, gain_v, load_sem,
    packed_taps, a_src, a_dst, b_src, b_mid, b_in, maps, x_src, x_by, x_on, x_in, z_src, z_by, z_on, z_in,
    w_src, w_all, mixed, weights, gat, gathered, sq_all,
    product, e_src, e_dst, d3_src, d3_dst,
    a_send, a_recv, b_send, b_recv, c_send, c_recv, x_send, x_recv, z_send, z_recv, w_send, w_recv,
    g_send, g_recv, f_send, f_recv, q_send, q_recv, e_send, e_recv, d3_send, d3_recv,
):
    rep = lax.axis_index("rep")
    samp = lax.axis_index("samp")
    tp = lax.axis_index("tp")
    low = tp // 8
    place = tp % 8
    across = place // 2
    core = place % 2
    group = tp // 4
    quarter = tp % 4

    def device(samp_index, tp_index):
        return (rep, samp_index, tp_index)

    pairs = (
        (group_ref, w_group), (prompt_ref, tokens.at[pl.ds(0, PROMPT)]), (fresh_ref, tokens.at[pl.ds(PROMPT, FRESH)]),
        (group_taps_ref, group_taps_v), (group_bias_ref, group_bias_v), (step_ref, w_step),
        (in_ref.at[1], w_in.at[1]), (in_ref.at[0], w_in.at[0]), (taps_ref, taps_v), (bias_ref, bias_v),
        (step_bias_ref, step_bias_v), (decay_ref, decay_v), (skip_ref, skip_v), (gain_ref, gain_v), (out_ref, w_out),
    )
    loads = [pltpu.make_async_copy(a, b, load_sem.at[i]) for i, (a, b) in enumerate(pairs)]
    for load in loads[:3]:
        load.start()

    barrier = pltpu.get_barrier_semaphore()

    def greet(samp_index, tp_index):
        pl.semaphore_signal(barrier, inc=1, device_id=device(samp_index, tp_index), device_id_type=MESH)

    for d in (2, 1, 3):
        greet((samp + d) % 4, tp)
    for i in range(4):
        @pl.when(jnp.logical_or(low != samp, i != low))
        def _():
            greet(low, i * 8 + place)
    for i in range(8):
        @pl.when(quarter * 8 + i != tp)
        def _():
            greet(samp, quarter * 8 + i)
    for d in range(1, 4):
        greet(samp, group * 4 + (quarter + d) % 4)
        greet(samp, low * 8 + ((across + d) % 4) * 2 + core)
        greet(samp, low * 8 + ((across + d) % 4) * 2 + 1 - core)

    for load in loads[3:]:
        load.start()
    sends = []

    def copy(source, target, send, recv, samp_index, tp_index):
        return pltpu.make_async_remote_copy(
            src_ref=source, dst_ref=target, send_sem=send, recv_sem=recv,
            device_id=device(samp_index, tp_index), device_id_type=MESH,
        )

    def start(copies):
        for one in copies:
            one.start()
            sends.append(one)
        return copies

    tokens[pl.ds(ROWS, PADDED - ROWS), :] = jnp.zeros((PADDED - ROWS, WIDTH), BF16)
    packed_taps[...] = jnp.zeros(packed_taps.shape, F32)
    mixed[pl.ds(ROWS, PADDED - ROWS), :] = jnp.zeros((PADDED - ROWS, 128), BF16)

    row = iota((64, 64), 0)
    col = iota((64, 64), 1)
    regroup = (col == (row % 8) * 8 + row // 8).astype(F32).astype(BF16)
    requarter = (col == ((row % 16) // 4) * 16 + (row // 16) * 4 + row % 4).astype(F32).astype(BF16)

    for load in loads[:5]:
        load.wait()
    for at, value in ((64, group_taps_v[...]), (68, group_bias_v[...])):
        high = value.astype(BF16).astype(F32)
        packed_taps[pl.ds(at, value.shape[0]), :] = high
        packed_taps[pl.ds(at + 8, value.shape[0]), :] = value - high
    maps_partial = mm_nt(w_group[...], tokens[...]).astype(BF16)
    regrouped = mm(regroup, maps_partial)
    tail = regrouped[:, PROMPT:] + mm_nt(regroup, packed_taps[...].astype(BF16))
    a_src[:, :, pl.ds(0, PROMPT)] = regrouped[:, :PROMPT].reshape(8, 8, PROMPT).astype(BF16)
    a_src[:, :, pl.ds(PROMPT, 128)] = tail.reshape(8, 8, 128).astype(BF16)

    pl.semaphore_wait(
        barrier, 22 + jnp.where(quarter != low, 1, 0) + jnp.where(samp != low, 1, 0)
    )

    def a_copy(g):
        return copy(a_src.at[g], a_dst.at[place], a_send.at[g], a_recv.at[place], samp, g * 4 + low)

    for g in range(8):
        @pl.when(g * 4 + low != tp)
        def _():
            a_copy(g).start()

        @pl.when(g * 4 + low == tp)
        def _():
            a_dst[pl.ds(place, 1)] = a_src[pl.ds(g, 1)]

    lane_h = iota((160, 128), 1)

    def packed(part, h):
        upper = part[:160, 128 * (h // 2):128 * (h // 2) + 128]
        lower = part[160:, 128 * (h // 2):128 * (h // 2) + 128]
        if h % 2 == 0:
            return jnp.where(lane_h < 64, upper, pltpu.roll(lower, 64, 1)).astype(BF16)
        return jnp.where(lane_h < 64, pltpu.roll(upper, 64, 1), lower).astype(BF16)

    above, below, opposite = (samp + 1) % 4, (samp + 3) % 4, (samp + 2) % 4

    def first_leg(source, by, into, send, recv):
        top, rest = pl.ds(0, BLOCK), pl.ds(BLOCK, source.shape[1] - BLOCK)
        return start([
            copy(source.at[opposite, top], by.at[top], send.at[0], recv.at[0], above, tp),
            copy(source.at[opposite, rest], by.at[rest], send.at[1], recv.at[1], below, tp),
            copy(source.at[above, rest], into.at[0, rest], send.at[2], recv.at[2], above, tp),
            copy(source.at[below, top], into.at[1, top], send.at[3], recv.at[3], below, tp),
        ])

    def second_leg(first, source, by, on, into, send, recv):
        top, rest = pl.ds(0, BLOCK), pl.ds(BLOCK, source.shape[1] - BLOCK)
        copies = []
        for i, (rows, to) in enumerate(((top, above), (rest, below))):
            first[i].wait_recv()
            on[rows, :] = (source[to, rows, :].astype(F32) + by[rows, :].astype(F32)).astype(BF16)
            copies += start([copy(on.at[rows], into.at[i, rows], send.at[4 + i], recv.at[4 + i], to, tp)])
        return first[2:] + copies

    loads[5].wait()
    sizes = mm_nt(w_step[...], tokens[...])
    loads[6].wait()
    head_part = mm(tokens[pl.ds(0, ROWS), :], w_in[1])
    size_row = iota((16, 128), 0)
    for h in range(4):
        x_src[h, pl.ds(0, 160), :] = packed(head_part, h)
        piece = jnp.zeros((16, 128), F32)
        for b in range(3):
            piece = jnp.where(size_row == b, sizes[h:h + 1, 128 * b:128 * b + 128], piece)
        x_src[h, pl.ds(160, 16), :] = piece.astype(BF16)
    x_copies = first_leg(x_src, x_by, x_in, x_send, x_recv)
    loads[7].wait()
    gate_part = mm(tokens[pl.ds(0, ROWS), :], w_in[0])
    for h in range(4):
        z_src[h] = packed(gate_part, h)

    for i in range(8):
        @pl.when(quarter * 8 + i != tp)
        def _():
            pltpu.make_async_copy(a_dst.at[i], a_dst.at[i], a_recv.at[i]).wait()
    own_maps = a_dst[...].astype(F32).reshape(64, PADDED)
    lane_q = iota((32, 128), 1)
    fresh_maps = own_maps[:, PROMPT:]
    b_src[pl.ds(0, 64), :] = own_maps[:, 0:128].astype(BF16)
    b_src[pl.ds(64, 64), :] = own_maps[:, 128:256].astype(BF16)
    b_src[pl.ds(128, 32), :] = jnp.where(lane_q < 64, fresh_maps[:32], pltpu.roll(fresh_maps[32:], 64, 1)).astype(BF16)
    pairings = (samp + 1 - 2 * (samp % 2), 3 - samp)
    b_rows = (pl.ds(0, BLOCK), pl.ds(BLOCK, BLOCK))

    def b_step(step, source):
        copies = []
        for i, rows in enumerate(b_rows):
            if step == 1:
                b_copies[i].wait_recv()
                b_mid[rows, :] = (b_src[rows, :].astype(F32) + b_in[0, rows, :].astype(F32)).astype(BF16)
            copies += start([
                copy(
                    source.at[rows], b_in.at[step, rows], b_send.at[step, i], b_recv.at[step, i],
                    pairings[(i + step) % 2], tp,
                )
            ])
        return copies

    b_copies = b_step(0, b_src)

    for load in loads[13:]:
        load.wait()
    gain = jnp.transpose(jnp.broadcast_to(gain_v[...], (128, CHANNELS)))
    for to in range(4):
        for part in range(4):
            columns = pl.ds(512 * to + 128 * part, 128)
            w_src[to, :, pl.ds(128 * part, 128)] = (w_out[:, columns].astype(F32) * gain).astype(BF16)
    w_all[pl.ds(across, 1)] = w_src[pl.ds(across, 1)]
    w_copies = start([
        copy(
            w_src.at[(across + d) % 4], w_all.at[across], w_send.at[d - 1], w_recv.at[d - 1],
            samp, low * 8 + ((across + d) % 4) * 2 + core,
        )
        for d in (2, 1, 3)
    ])

    x_copies = second_leg(x_copies, x_src, x_by, x_on, x_in, x_send, x_recv)
    b_copies = b_step(1, b_mid)
    z_copies = first_leg(z_src, z_by, z_in, z_send, z_recv)

    lane128 = iota((1, 128), 1)

    def of_head(value):
        chosen = jnp.zeros((value.shape[0], 128), F32)
        for h in range(4):
            half = value[:, 128 * (h // 2):128 * (h // 2) + 128]
            if h % 2 == 0:
                half = pltpu.roll(half, 64, 1)
            chosen = jnp.where(samp == h, half, chosen)
        return jnp.where(lane128 >= 64, chosen, 0.0)

    def own_scalar(ref):
        return jnp.sum(jnp.where(iota((1, 4), 1) == samp, ref[...], 0.0), axis=1, keepdims=True)

    def unpacked(value):
        return jnp.concatenate([pltpu.roll(value, 64, 1), value], axis=0)

    for load in loads[8:13]:
        load.wait()
    taps8 = of_head(jnp.concatenate([taps_v[...], bias_v[...], jnp.zeros((3, CHANNELS), F32)], axis=0))
    skip = own_scalar(skip_v)
    step_bias = own_scalar(step_bias_v)
    rate = jnp.exp(own_scalar(decay_v))
    z_copies = second_leg(z_copies, z_src, z_by, z_on, z_in, z_send, z_recv)
    for one in x_copies:
        one.wait_recv()
    summed = x_src[samp].astype(F32) + x_in[0].astype(F32) + x_in[1].astype(F32)
    summed = summed.astype(BF16).astype(F32)
    heads = unpacked(summed[:160])
    before = heads[:PROMPT]
    row_p = iota((PROMPT, 128), 0)
    conv = taps8[4:5] + taps8[3:4] * before
    for k in range(1, 4):
        conv = conv + taps8[3 - k:4 - k] * jnp.where(row_p >= k, pltpu.roll(before, k, 0), 0.0)
    mixed[pl.ds(0, PROMPT), :] = silu(conv).astype(BF16)
    line = jnp.concatenate(
        [jnp.broadcast_to(before[253 + k:254 + k], (16, 128)) for k in range(3)] + [heads[PROMPT:ROWS]], axis=0
    )
    conv = taps8[4:5] + taps8[0:1] * line[0:64]
    for k in range(1, 4):
        conv = conv + taps8[k:k + 1] * line[16 * k:16 * k + 64]
    mixed[pl.ds(PROMPT, FRESH), :] = silu(conv).astype(BF16)

    size = jnp.concatenate([summed[160 + b:161 + b] for b in range(3)], axis=1)
    size = jnp.broadcast_to(size, (8, PADDED)) + step_bias
    size = jnp.maximum(size, 0.0) + jnp.log1p(jnp.exp(-jnp.abs(size)))
    logs = -size * rate
    run = logs[:, :PROMPT]
    lane_r = iota((8, PROMPT), 1)
    for k in (1, 2, 4, 8, 16, 32, 64, 128):
        run = run + jnp.where(lane_r >= k, pltpu.roll(run, k, 1), 0.0)
    run_f = logs[:, PROMPT:]
    lane_s = iota((8, 128), 1)
    for k in (16, 32):
        run_f = run_f + jnp.where(lane_s >= k, pltpu.roll(run_f, k, 1), 0.0)
    run_f = run_f + run[:, PROMPT - 1:PROMPT]
    runs = [run[0:1, 0:128], run[0:1, 128:256], run_f[0:1]]
    trail = jnp.concatenate([jnp.transpose(jnp.broadcast_to(r, (128, 128))) for r in runs], axis=0)[:ROWS]
    lane = iota((128, 128), 1)
    row_q = iota((128, 128), 0)
    tiles = ((256, 64, 0), (256, 64, 1), (256, 64, 2), (0, 128, 0), (128, 128, 0), (128, 128, 1))
    offsets = (0, 64, 128, 192, 320, 448)
    for (first, count, b), offset in zip(tiles, offsets):
        gap = trail[first:first + count] - runs[b]
        if b == 2:
            seen = jnp.logical_and(lane <= row_q, lane % 16 == row_q % 16)[:count]
            gap = jnp.where(seen, gap, -1e30)
        elif first == 128 * b:
            gap = jnp.where(lane <= row_q, gap, -1e30)
        weights[pl.ds(offset, count), :] = jnp.exp(gap) * size[0:1, 128 * b:128 * b + 128]

    for one in b_copies:
        one.wait_recv()
    total = b_mid[...].astype(F32) + b_in[1].astype(F32)
    total = total.astype(BF16).astype(F32)
    taps = [own_maps[:, 320 + k:321 + k] + own_maps[:, 328 + k:329 + k] for k in range(5)]
    before = jnp.concatenate([total[0:64], total[64:128]], axis=1)
    lane_p = iota((64, PROMPT), 1)
    conv = taps[4] + taps[3] * before
    for k in range(1, 4):
        conv = conv + taps[3 - k] * jnp.where(lane_p >= k, pltpu.roll(before, k, 1), 0.0)
    maps_prompt = silu(conv).astype(BF16)
    lane_f = iota((64, 128), 1)
    line = jnp.concatenate([total[128:160], pltpu.roll(total[128:160], 64, 1)], axis=0)
    line = pltpu.roll(line, 48, 1)
    for k in range(3):
        line = jnp.where(
            jnp.logical_and(lane_f >= 16 * k, lane_f < 16 * k + 16), before[:, 253 + k:254 + k], line
        )
    conv = taps[4] + taps[0] * line
    for k in range(1, 4):
        conv = conv + taps[k] * pltpu.roll(line, 128 - 16 * k, 1)
    maps_fresh = jnp.where(lane_f < 64, silu(conv), 0.0).astype(BF16)
    maps[quarter, :, pl.ds(0, PROMPT)] = maps_prompt
    maps[quarter, :, pl.ds(PROMPT, 128)] = maps_fresh
    c_copies = start([
        copy(maps.at[quarter], maps.at[quarter], c_send.at[d - 1], c_recv.at[d - 1], samp, group * 4 + (quarter + d) % 4)
        for d in (3, 2, 1)
    ])
    for one in c_copies:
        one.wait_recv()
    inputs = jnp.concatenate([maps[0], maps[1]], axis=0)
    to_read = jnp.concatenate([maps[2], maps[3]], axis=0).astype(F32)
    readout = jnp.transpose(to_read).astype(BF16)

    def read(first, count, blocks):
        value = skip * mixed[pl.ds(first, count), :].astype(F32)
        for b, offset in blocks:
            products = mm(readout[first:first + count], inputs[:, 128 * b:128 * b + 128])
            seen = (weights[pl.ds(offset, count), :] * products).astype(BF16)
            value = value + mm(seen, mixed[pl.ds(128 * b, 128), :])
        return value

    fresh = read(256, 64, ((0, 0), (1, 64), (2, 128)))
    halves = [read(0, 128, ((0, 192),)), read(128, 128, ((0, 320), (1, 448)))]
    for one in z_copies:
        one.wait_recv()
    gate = z_src[samp].astype(F32) + z_in[0].astype(F32) + z_in[1].astype(F32)
    gate = silu(unpacked(gate.astype(BF16).astype(F32)))
    fresh = mm(requarter, (fresh * gate[PROMPT:]).astype(BF16))

    lane_c = iota((BLOCK, 128), 1)

    def onward(c, k):
        piece = (samp - k + 4) % 4
        return start([
            copy(
                gat.at[c, across, piece], gat.at[c, across, piece], f_send.at[c, k, d - 1], f_recv.at[c, k, d - 1],
                samp, low * 8 + ((across + d) % 4) * 2 + core,
            )
            for d in (2, 1, 3)
        ])

    for c in range(2):
        gated = halves[c] * gate[128 * c:128 * c + 128]
        upper = jnp.concatenate([gated[:64], fresh[32 * c:32 * c + 16]], axis=0)
        lower = jnp.concatenate([gated[64:], fresh[32 * c + 16:32 * c + 32]], axis=0)
        gat[c, across, samp] = jnp.where(lane_c < 64, pltpu.roll(upper, 64, 1), lower).astype(BF16)
    g_copies = [{}, {}]
    for d in (2, 1, 3):
        for c in range(2):
            g_copies[c][d] = start([
                copy(
                    gat.at[c, across, samp], gat.at[c, across, samp], g_send.at[c, d - 1], g_recv.at[c, d - 1],
                    (samp + d) % 4, tp,
                )
            ])[0]
    f_copies = [onward(c, 0) for c in range(2)]
    for k in (1, 3, 2):
        for c in range(2):
            g_copies[c][k].wait_recv()
            f_copies[c] += onward(c, k)

    def side_by_side(c, at, pair):
        first, second = gat[c, at, 2 * pair].astype(F32), gat[c, at, 2 * pair + 1].astype(F32)
        return jnp.concatenate([
            jnp.where(lane_c < 64, first, pltpu.roll(second, 64, 1)),
            jnp.where(lane_c < 64, pltpu.roll(first, 64, 1), second),
        ], axis=0)

    squares = []
    for c in range(2):
        parts = [side_by_side(c, across, pair) for pair in range(2)]
        squares.append(jnp.sum(parts[0] * parts[0] + parts[1] * parts[1], axis=1, keepdims=True))
    squares = jnp.concatenate(squares + [jnp.zeros((PADDED - ROWS, 1), F32)], axis=0)
    sq_all[place] = jnp.transpose(jnp.broadcast_to(squares, (PADDED, 128)))[0:1]

    def q_copy(i):
        return copy(sq_all.at[place], sq_all.at[place], q_send.at[i], q_recv.at[place], samp, low * 8 + i)

    for i in range(8):
        @pl.when(place != i)
        def _():
            q_copy(i).start()

    for one in w_copies:
        one.wait_recv()
    e_copies = []
    for c in range(2):
        for one in f_copies[c]:
            one.wait_recv()
        for at in range(4):
            for pair in range(2):
                gathered[:, pl.ds(256 * at + 128 * pair, 128)] = side_by_side(c, at, pair).astype(BF16)
        products = [
            mm(gathered[:, pl.ds(512 * half, 512)], w_all[2 * half:2 * half + 2].reshape(512, 512)) for half in range(2)
        ]
        if c == 0:
            for i in range(8):
                @pl.when(place != i)
                def _():
                    pltpu.make_async_copy(sq_all.at[i], sq_all.at[i], q_recv.at[i]).wait()
            scales = []
            for half in range(2):
                total = sq_all[4 * half] + sq_all[4 * half + 1] + sq_all[4 * half + 2] + sq_all[4 * half + 3]
                scale = jnp.broadcast_to(lax.rsqrt(total * (1.0 / 1024.0) + 1e-5), (128, PADDED))
                scales.append(jnp.transpose(scale))
        scaled = [
            products[half] * jnp.concatenate([scales[half][2 * BLOCK * c:2 * BLOCK * c + 2 * BLOCK]] * 4, axis=1)
            for half in range(2)
        ]
        scaled = scaled[0] + scaled[1]
        product[c, 0] = scaled[:, :256]
        product[c, 1] = scaled[:, 256:]
        e_src[c] = product[c, 1 - core].astype(BF16)
        e_copies += start([
            copy(e_src.at[c], e_dst.at[c], e_send.at[c], e_recv.at[c], samp, low * 8 + across * 2 + 1 - core)
        ])

    def d3_copy(s):
        return copy(d3_src.at[s], d3_dst.at[low], d3_send.at[s], d3_recv.at[low], s, samp * 8 + place)

    def stays(s):
        return jnp.logical_and(samp == low, samp == s)

    for c in range(2):
        e_copies[c].wait_recv()
        outer = jnp.logical_or(samp == 0, samp == 3)
        far = jnp.where(outer, 1 - c, c)
        for half in (far, 1 - far):
            rows = pl.ds(pl.multiple_of(BLOCK * half, 16), BLOCK)
            s = 2 * c + half
            d3_src[s] = (product[c, core, rows, :] + e_dst[c, rows, :].astype(F32)).astype(BF16)

            @pl.when(stays(s))
            def _():
                d3_dst[low] = d3_src[s]

            @pl.when(jnp.logical_not(stays(s)))
            def _():
                d3_copy(s).start()

    for i in range(4):
        @pl.when(jnp.logical_or(low != samp, i != low))
        def _():
            pltpu.make_async_copy(d3_dst.at[i], d3_dst.at[i], d3_recv.at[i]).wait()
    value = d3_dst[0].astype(F32)
    for i in range(1, 4):
        value = value + d3_dst[i].astype(F32)
    rows_ref[...] = value.astype(BF16)

    for i in range(8):
        @pl.when(place != i)
        def _():
            q_copy(i).wait_send()
    for g in range(8):
        @pl.when(g * 4 + low != tp)
        def _():
            a_copy(g).wait_send()
    for one in sends:
        one.wait_send()
    for s in range(4):
        @pl.when(jnp.logical_not(stays(s)))
        def _():
            d3_copy(s).wait_send()


def finish(rows_ref, lengths_ref, prefill_ref, decode_ref):
    prefill_ref[...] = rows_ref[:64]
    step = iota((16, CHANNELS), 0)
    lengths = jnp.zeros((16, CHANNELS), jnp.int32)
    for i in range(4):
        lengths = jnp.where(step % 4 == i, lengths_ref[0, i], lengths)
    decode = jnp.where(step // 4 < lengths, rows_ref[64:].astype(F32), 0.0).astype(BF16)
    for i in range(4):
        decode_ref[i] = decode[4 * i:4 * i + 4]


def shards(
    prompt_tokens, step_tokens, lengths, input_weight, group_weight, step_weight,
    conv_weight, group_conv, conv_bias, group_bias, step_bias, decay_log, skip_gain, norm_gain, output_weight,
):
    anywhere = pl.BlockSpec(memory_space=pl.ANY)
    vector = pl.BlockSpec(memory_space=pltpu.VMEM)

    def dma(*shape):
        return pltpu.SemaphoreType.DMA(shape)

    def room(*shape):
        return pltpu.VMEM(shape, BF16)

    def wide_room(*shape):
        return pltpu.VMEM(shape, F32)

    rows = pl.pallas_call(
        kernel,
        out_shape=jax.ShapeDtypeStruct((BLOCK, CHANNELS), BF16),
        in_specs=[anywhere] * 14,
        out_specs=vector,
        scratch_shapes=[
            room(PADDED, WIDTH), room(2, WIDTH, CHANNELS), room(64, WIDTH), room(CHANNELS, WIDTH), room(4, WIDTH),
            wide_room(4, CHANNELS), wide_room(1, CHANNELS), wide_room(4, 64), wide_room(1, 64),
            wide_room(1, 4), wide_room(1, 4), wide_room(1, 4), wide_room(1, CHANNELS), dma(15),
            wide_room(128, 64),
            room(8, 8, PADDED), room(8, 8, PADDED),
            room(160, 128), room(160, 128), room(2, 160, 128),
            room(4, 64, PADDED),
            room(4, 176, 128), room(176, 128), room(176, 128), room(2, 176, 128),
            room(4, 160, 128), room(160, 128), room(160, 128), room(2, 160, 128),
            room(4, CHANNELS, 512), room(4, CHANNELS, 512),
            room(PADDED, 128), wide_room(576, 128),
            room(2, 4, 4, BLOCK, 128), room(2 * BLOCK, 1024), wide_room(8, 1, PADDED),
            wide_room(2, 2, 2 * BLOCK, CHANNELS), room(2, 2 * BLOCK, CHANNELS), room(2, 2 * BLOCK, CHANNELS),
            room(4, BLOCK, CHANNELS), room(4, BLOCK, CHANNELS),
            dma(8), dma(8), dma(2, 2), dma(2, 2), dma(3), dma(3), dma(6), dma(6), dma(6), dma(6), dma(3), dma(3),
            dma(2, 3), dma(2, 3), dma(2, 4, 3), dma(2, 4, 3), dma(8), dma(8), dma(2), dma(2), dma(4), dma(4),
        ],
        compiler_params=pltpu.CompilerParams(
            collective_id=0, has_side_effects=True, vmem_limit_bytes=VMEM_LIMIT
        ),
        cost_estimate=pl.CostEstimate(flops=2 * 10**9, bytes_accessed=8 * 10**6, transcendentals=10**6),
    )(
        prompt_tokens.reshape(PROMPT, WIDTH),
        step_tokens.reshape(FRESH, WIDTH),
        input_weight,
        group_weight.T,
        output_weight,
        step_weight.T,
        conv_weight,
        conv_bias.reshape(1, CHANNELS),
        group_conv,
        group_bias.reshape(1, 64),
        step_bias.reshape(1, 4),
        decay_log.reshape(1, 4),
        skip_gain.reshape(1, 4),
        norm_gain.reshape(1, CHANNELS),
    )
    prefill, decode = pl.pallas_call(
        finish,
        out_shape=(
            jax.ShapeDtypeStruct((64, CHANNELS), BF16),
            jax.ShapeDtypeStruct((4, 4, CHANNELS), BF16),
        ),
        in_specs=[vector, pl.BlockSpec(memory_space=pltpu.SMEM)],
        out_specs=(vector, vector),
    )(rows, lengths.reshape(1, 4))
    return prefill[:, None, :], decode[:, :, None, :]


def solution(mesh):
    placed = (
        P(None, "rep", "samp"),
        P(None, None, "rep", "samp"),
        P("samp", "rep"),
        P(None, "samp", "tp"),
        P("samp", "tp"),
        P("samp", "tp"),
        P(None, "tp"),
        P(None, "tp"),
        P("tp"),
        P("tp"),
        P("tp"),
        P("tp"),
        P("tp"),
        P("tp"),
        P("tp", "samp"),
    )
    return jax.shard_map(
        shards,
        mesh=mesh,
        in_specs=placed,
        out_specs=(P("samp", "rep", "tp"), P(None, "samp", "rep", "tp")),
        check_vma=False,
    )
```

```python
import jax
import jax.numpy as jnp
from jax import lax
from jax.experimental import pallas as pl
from jax.experimental.pallas import tpu as pltpu
from jax.sharding import PartitionSpec as P

PROMPT = 256
FRESH = 64
ROWS = 320
PADDED = 384
WIDTH = 2048
CHANNELS = 256
BLOCK = 80
VMEM_LIMIT = 60 * 1024 * 1024
MESH = pl.DeviceIdType.MESH
F32 = jnp.float32
BF16 = jnp.bfloat16
NT = (((1,), (1,)), ((), ()))


def mm(a, b):
    return jnp.dot(a, b, preferred_element_type=F32)


def mm_nt(a, b):
    return lax.dot_general(a, b, NT, preferred_element_type=F32)


def iota(shape, axis):
    return lax.broadcasted_iota(jnp.int32, shape, axis)


def silu(v):
    return v / (1.0 + jnp.exp(-v))


def kernel(
    prompt_ref, fresh_ref, in_ref, group_ref, out_ref, step_ref, taps_ref, bias_ref,
    group_taps_ref, group_bias_ref, step_bias_ref, decay_ref, skip_ref, gain_ref,
    rows_ref,
    tokens, w_in, w_group, w_out, w_step, taps_v, bias_v, group_taps_v, group_bias_v,
    step_bias_v, decay_v, skip_v, gain_v, load_sem,
    packed_taps, a_src, a_dst, b_src, b_mid, b_in, maps, x_src, x_by, x_on, x_in, z_src, z_by, z_on, z_in,
    w_src, w_all, mixed, weights, gat, gathered, sq_all,
    product, e_src, e_dst, d3_src, d3_dst,
    a_send, a_recv, b_send, b_recv, c_send, c_recv, x_send, x_recv, z_send, z_recv, w_send, w_recv,
    g_send, g_recv, f_send, f_recv, q_send, q_recv, e_send, e_recv, d3_send, d3_recv,
):
    rep = lax.axis_index("rep")
    samp = lax.axis_index("samp")
    tp = lax.axis_index("tp")
    low = tp // 8
    place = tp % 8
    across = place // 2
    core = place % 2
    group = tp // 4
    quarter = tp % 4

    def device(samp_index, tp_index):
        return (rep, samp_index, tp_index)

    pairs = (
        (group_ref, w_group), (prompt_ref, tokens.at[pl.ds(0, PROMPT)]), (fresh_ref, tokens.at[pl.ds(PROMPT, FRESH)]),
        (group_taps_ref, group_taps_v), (group_bias_ref, group_bias_v), (step_ref, w_step),
        (in_ref.at[1], w_in.at[1]), (in_ref.at[0], w_in.at[0]), (taps_ref, taps_v), (bias_ref, bias_v),
        (step_bias_ref, step_bias_v), (decay_ref, decay_v), (skip_ref, skip_v), (gain_ref, gain_v), (out_ref, w_out),
    )
    loads = [pltpu.make_async_copy(a, b, load_sem.at[i]) for i, (a, b) in enumerate(pairs)]
    for load in loads[:3]:
        load.start()

    barrier = pltpu.get_barrier_semaphore()

    def greet(samp_index, tp_index):
        pl.semaphore_signal(barrier, inc=1, device_id=device(samp_index, tp_index), device_id_type=MESH)

    for d in (2, 1, 3):
        greet((samp + d) % 4, tp)
    for i in range(4):
        @pl.when(jnp.logical_or(low != samp, i != low))
        def _():
            greet(low, i * 8 + place)
    for i in range(8):
        @pl.when(quarter * 8 + i != tp)
        def _():
            greet(samp, quarter * 8 + i)
    for d in range(1, 4):
        greet(samp, group * 4 + (quarter + d) % 4)
        greet(samp, low * 8 + ((across + d) % 4) * 2 + core)
        greet(samp, low * 8 + ((across + d) % 4) * 2 + 1 - core)

    for load in loads[3:]:
        load.start()
    sends = []

    def copy(source, target, send, recv, samp_index, tp_index):
        return pltpu.make_async_remote_copy(
            src_ref=source, dst_ref=target, send_sem=send, recv_sem=recv,
            device_id=device(samp_index, tp_index), device_id_type=MESH,
        )

    def start(copies):
        for one in copies:
            one.start()
            sends.append(one)
        return copies

    tokens[pl.ds(ROWS, PADDED - ROWS), :] = jnp.zeros((PADDED - ROWS, WIDTH), BF16)
    packed_taps[...] = jnp.zeros(packed_taps.shape, F32)
    mixed[pl.ds(ROWS, PADDED - ROWS), :] = jnp.zeros((PADDED - ROWS, 128), BF16)

    row = iota((64, 64), 0)
    col = iota((64, 64), 1)
    regroup = (col == (row % 8) * 8 + row // 8).astype(F32).astype(BF16)
    requarter = (col == ((row % 16) // 4) * 16 + (row // 16) * 4 + row % 4).astype(F32).astype(BF16)

    for load in loads[:5]:
        load.wait()
    for at, value in ((64, group_taps_v[...]), (68, group_bias_v[...])):
        high = value.astype(BF16).astype(F32)
        packed_taps[pl.ds(at, value.shape[0]), :] = high
        packed_taps[pl.ds(at + 8, value.shape[0]), :] = value - high
    maps_partial = mm_nt(w_group[...], tokens[...]).astype(BF16)
    regrouped = mm(regroup, maps_partial)
    tail = regrouped[:, PROMPT:] + mm_nt(regroup, packed_taps[...].astype(BF16))
    a_src[:, :, pl.ds(0, PROMPT)] = regrouped[:, :PROMPT].reshape(8, 8, PROMPT).astype(BF16)
    a_src[:, :, pl.ds(PROMPT, 128)] = tail.reshape(8, 8, 128).astype(BF16)

    pl.semaphore_wait(
        barrier, 22 + jnp.where(quarter != low, 1, 0) + jnp.where(samp != low, 1, 0)
    )

    def a_copy(g):
        return copy(a_src.at[g], a_dst.at[place], a_send.at[g], a_recv.at[place], samp, g * 4 + low)

    for g in range(8):
        @pl.when(g * 4 + low != tp)
        def _():
            a_copy(g).start()

        @pl.when(g * 4 + low == tp)
        def _():
            a_dst[pl.ds(place, 1)] = a_src[pl.ds(g, 1)]

    lane_h = iota((160, 128), 1)

    def packed(part, h):
        upper = part[:160, 128 * (h // 2):128 * (h // 2) + 128]
        lower = part[160:, 128 * (h // 2):128 * (h // 2) + 128]
        if h % 2 == 0:
            return jnp.where(lane_h < 64, upper, pltpu.roll(lower, 64, 1)).astype(BF16)
        return jnp.where(lane_h < 64, pltpu.roll(upper, 64, 1), lower).astype(BF16)

    above, below, opposite = (samp + 1) % 4, (samp + 3) % 4, (samp + 2) % 4

    def first_leg(source, by, into, send, recv):
        top, rest = pl.ds(0, BLOCK), pl.ds(BLOCK, source.shape[1] - BLOCK)
        return start([
            copy(source.at[opposite, top], by.at[top], send.at[0], recv.at[0], above, tp),
            copy(source.at[opposite, rest], by.at[rest], send.at[1], recv.at[1], below, tp),
            copy(source.at[above, rest], into.at[0, rest], send.at[2], recv.at[2], above, tp),
            copy(source.at[below, top], into.at[1, top], send.at[3], recv.at[3], below, tp),
        ])

    def second_leg(first, source, by, on, into, send, recv):
        top, rest = pl.ds(0, BLOCK), pl.ds(BLOCK, source.shape[1] - BLOCK)
        copies = []
        for i, (rows, to) in enumerate(((top, above), (rest, below))):
            first[i].wait_recv()
            on[rows, :] = (source[to, rows, :].astype(F32) + by[rows, :].astype(F32)).astype(BF16)
            copies += start([copy(on.at[rows], into.at[i, rows], send.at[4 + i], recv.at[4 + i], to, tp)])
        return first[2:] + copies

    loads[5].wait()
    sizes = mm_nt(w_step[...], tokens[...])
    loads[6].wait()
    head_part = mm(tokens[pl.ds(0, ROWS), :], w_in[1])
    size_row = iota((16, 128), 0)
    for h in range(4):
        x_src[h, pl.ds(0, 160), :] = packed(head_part, h)
        piece = jnp.zeros((16, 128), F32)
        for b in range(3):
            piece = jnp.where(size_row == b, sizes[h:h + 1, 128 * b:128 * b + 128], piece)
        x_src[h, pl.ds(160, 16), :] = piece.astype(BF16)
    x_copies = first_leg(x_src, x_by, x_in, x_send, x_recv)
    for load in loads[13:]:
        load.wait()
    gain = jnp.transpose(jnp.broadcast_to(gain_v[...], (128, CHANNELS)))
    for to in range(4):
        for part in range(4):
            columns = pl.ds(512 * to + 128 * part, 128)
            w_src[to, :, pl.ds(128 * part, 128)] = (w_out[:, columns].astype(F32) * gain).astype(BF16)
    w_all[pl.ds(across, 1)] = w_src[pl.ds(across, 1)]
    w_copies = start([
        copy(
            w_src.at[(across + d) % 4], w_all.at[across], w_send.at[d - 1], w_recv.at[d - 1],
            samp, low * 8 + ((across + d) % 4) * 2 + core,
        )
        for d in (2, 1, 3)
    ])

    loads[7].wait()
    gate_part = mm(tokens[pl.ds(0, ROWS), :], w_in[0])
    for h in range(4):
        z_src[h] = packed(gate_part, h)

    for i in range(8):
        @pl.when(quarter * 8 + i != tp)
        def _():
            pltpu.make_async_copy(a_dst.at[i], a_dst.at[i], a_recv.at[i]).wait()
    own_maps = a_dst[...].astype(F32).reshape(64, PADDED)
    lane_q = iota((32, 128), 1)
    fresh_maps = own_maps[:, PROMPT:]
    b_src[pl.ds(0, 64), :] = own_maps[:, 0:128].astype(BF16)
    b_src[pl.ds(64, 64), :] = own_maps[:, 128:256].astype(BF16)
    b_src[pl.ds(128, 32), :] = jnp.where(lane_q < 64, fresh_maps[:32], pltpu.roll(fresh_maps[32:], 64, 1)).astype(BF16)
    pairings = (samp + 1 - 2 * (samp % 2), 3 - samp)
    b_rows = (pl.ds(0, BLOCK), pl.ds(BLOCK, BLOCK))

    def b_step(step, source):
        copies = []
        for i, rows in enumerate(b_rows):
            if step == 1:
                b_copies[i].wait_recv()
                b_mid[rows, :] = (b_src[rows, :].astype(F32) + b_in[0, rows, :].astype(F32)).astype(BF16)
            copies += start([
                copy(
                    source.at[rows], b_in.at[step, rows], b_send.at[step, i], b_recv.at[step, i],
                    pairings[(i + step) % 2], tp,
                )
            ])
        return copies

    b_copies = b_step(0, b_src)

    x_copies = second_leg(x_copies, x_src, x_by, x_on, x_in, x_send, x_recv)
    b_copies = b_step(1, b_mid)
    z_copies = first_leg(z_src, z_by, z_in, z_send, z_recv)

    lane128 = iota((1, 128), 1)

    def of_head(value):
        chosen = jnp.zeros((value.shape[0], 128), F32)
        for h in range(4):
            half = value[:, 128 * (h // 2):128 * (h // 2) + 128]
            if h % 2 == 0:
                half = pltpu.roll(half, 64, 1)
            chosen = jnp.where(samp == h, half, chosen)
        return jnp.where(lane128 >= 64, chosen, 0.0)

    def own_scalar(ref):
        return jnp.sum(jnp.where(iota((1, 4), 1) == samp, ref[...], 0.0), axis=1, keepdims=True)

    def unpacked(value):
        return jnp.concatenate([pltpu.roll(value, 64, 1), value], axis=0)

    for load in loads[8:13]:
        load.wait()
    taps8 = of_head(jnp.concatenate([taps_v[...], bias_v[...], jnp.zeros((3, CHANNELS), F32)], axis=0))
    skip = own_scalar(skip_v)
    step_bias = own_scalar(step_bias_v)
    rate = jnp.exp(own_scalar(decay_v))
    z_copies = second_leg(z_copies, z_src, z_by, z_on, z_in, z_send, z_recv)
    for one in x_copies:
        one.wait_recv()
    summed = x_src[samp].astype(F32) + x_in[0].astype(F32) + x_in[1].astype(F32)
    summed = summed.astype(BF16).astype(F32)
    heads = unpacked(summed[:160])
    before = heads[:PROMPT]
    row_p = iota((PROMPT, 128), 0)
    conv = taps8[4:5] + taps8[3:4] * before
    for k in range(1, 4):
        conv = conv + taps8[3 - k:4 - k] * jnp.where(row_p >= k, pltpu.roll(before, k, 0), 0.0)
    mixed[pl.ds(0, PROMPT), :] = silu(conv).astype(BF16)
    line = jnp.concatenate(
        [jnp.broadcast_to(before[253 + k:254 + k], (16, 128)) for k in range(3)] + [heads[PROMPT:ROWS]], axis=0
    )
    conv = taps8[4:5] + taps8[0:1] * line[0:64]
    for k in range(1, 4):
        conv = conv + taps8[k:k + 1] * line[16 * k:16 * k + 64]
    mixed[pl.ds(PROMPT, FRESH), :] = silu(conv).astype(BF16)

    size = jnp.concatenate([summed[160 + b:161 + b] for b in range(3)], axis=1)
    size = jnp.broadcast_to(size, (8, PADDED)) + step_bias
    size = jnp.maximum(size, 0.0) + jnp.log1p(jnp.exp(-jnp.abs(size)))
    logs = -size * rate
    run = logs[:, :PROMPT]
    lane_r = iota((8, PROMPT), 1)
    for k in (1, 2, 4, 8, 16, 32, 64, 128):
        run = run + jnp.where(lane_r >= k, pltpu.roll(run, k, 1), 0.0)
    run_f = logs[:, PROMPT:]
    lane_s = iota((8, 128), 1)
    for k in (16, 32):
        run_f = run_f + jnp.where(lane_s >= k, pltpu.roll(run_f, k, 1), 0.0)
    run_f = run_f + run[:, PROMPT - 1:PROMPT]
    runs = [run[0:1, 0:128], run[0:1, 128:256], run_f[0:1]]
    trail = jnp.concatenate([jnp.transpose(jnp.broadcast_to(r, (128, 128))) for r in runs], axis=0)[:ROWS]
    lane = iota((128, 128), 1)
    row_q = iota((128, 128), 0)
    tiles = ((256, 64, 0), (256, 64, 1), (256, 64, 2), (0, 128, 0), (128, 128, 0), (128, 128, 1))
    offsets = (0, 64, 128, 192, 320, 448)
    for (first, count, b), offset in zip(tiles, offsets):
        gap = trail[first:first + count] - runs[b]
        if b == 2:
            seen = jnp.logical_and(lane <= row_q, lane % 16 == row_q % 16)[:count]
            gap = jnp.where(seen, gap, -1e30)
        elif first == 128 * b:
            gap = jnp.where(lane <= row_q, gap, -1e30)
        weights[pl.ds(offset, count), :] = jnp.exp(gap) * size[0:1, 128 * b:128 * b + 128]

    for one in b_copies:
        one.wait_recv()
    total = b_mid[...].astype(F32) + b_in[1].astype(F32)
    total = total.astype(BF16).astype(F32)
    taps = [own_maps[:, 320 + k:321 + k] + own_maps[:, 328 + k:329 + k] for k in range(5)]
    before = jnp.concatenate([total[0:64], total[64:128]], axis=1)
    lane_p = iota((64, PROMPT), 1)
    conv = taps[4] + taps[3] * before
    for k in range(1, 4):
        conv = conv + taps[3 - k] * jnp.where(lane_p >= k, pltpu.roll(before, k, 1), 0.0)
    maps_prompt = silu(conv).astype(BF16)
    lane_f = iota((64, 128), 1)
    line = jnp.concatenate([total[128:160], pltpu.roll(total[128:160], 64, 1)], axis=0)
    line = pltpu.roll(line, 48, 1)
    for k in range(3):
        line = jnp.where(
            jnp.logical_and(lane_f >= 16 * k, lane_f < 16 * k + 16), before[:, 253 + k:254 + k], line
        )
    conv = taps[4] + taps[0] * line
    for k in range(1, 4):
        conv = conv + taps[k] * pltpu.roll(line, 128 - 16 * k, 1)
    maps_fresh = jnp.where(lane_f < 64, silu(conv), 0.0).astype(BF16)
    maps[quarter, :, pl.ds(0, PROMPT)] = maps_prompt
    maps[quarter, :, pl.ds(PROMPT, 128)] = maps_fresh
    c_copies = start([
        copy(maps.at[quarter], maps.at[quarter], c_send.at[d - 1], c_recv.at[d - 1], samp, group * 4 + (quarter + d) % 4)
        for d in (3, 2, 1)
    ])
    for one in c_copies:
        one.wait_recv()
    inputs = jnp.concatenate([maps[0], maps[1]], axis=0)
    to_read = jnp.concatenate([maps[2], maps[3]], axis=0).astype(F32)
    readout = jnp.transpose(to_read).astype(BF16)

    def read(first, count, blocks):
        value = skip * mixed[pl.ds(first, count), :].astype(F32)
        for b, offset in blocks:
            products = mm(readout[first:first + count], inputs[:, 128 * b:128 * b + 128])
            seen = (weights[pl.ds(offset, count), :] * products).astype(BF16)
            value = value + mm(seen, mixed[pl.ds(128 * b, 128), :])
        return value

    fresh = read(256, 64, ((0, 0), (1, 64), (2, 128)))
    halves = [read(0, 128, ((0, 192),)), read(128, 128, ((0, 320), (1, 448)))]
    for one in z_copies:
        one.wait_recv()
    gate = z_src[samp].astype(F32) + z_in[0].astype(F32) + z_in[1].astype(F32)
    gate = silu(unpacked(gate.astype(BF16).astype(F32)))
    fresh = mm(requarter, (fresh * gate[PROMPT:]).astype(BF16))

    lane_c = iota((BLOCK, 128), 1)

    def onward(c, k):
        piece = (samp - k + 4) % 4
        return start([
            copy(
                gat.at[c, across, piece], gat.at[c, across, piece], f_send.at[c, k, d - 1], f_recv.at[c, k, d - 1],
                samp, low * 8 + ((across + d) % 4) * 2 + core,
            )
            for d in (2, 1, 3)
        ])

    for c in range(2):
        gated = halves[c] * gate[128 * c:128 * c + 128]
        upper = jnp.concatenate([gated[:64], fresh[32 * c:32 * c + 16]], axis=0)
        lower = jnp.concatenate([gated[64:], fresh[32 * c + 16:32 * c + 32]], axis=0)
        gat[c, across, samp] = jnp.where(lane_c < 64, pltpu.roll(upper, 64, 1), lower).astype(BF16)
    g_copies = [{}, {}]
    for d in (2, 1, 3):
        for c in range(2):
            g_copies[c][d] = start([
                copy(
                    gat.at[c, across, samp], gat.at[c, across, samp], g_send.at[c, d - 1], g_recv.at[c, d - 1],
                    (samp + d) % 4, tp,
                )
            ])[0]
    f_copies = [onward(c, 0) for c in range(2)]
    for k in (1, 3, 2):
        for c in range(2):
            g_copies[c][k].wait_recv()
            f_copies[c] += onward(c, k)

    def side_by_side(c, at, pair):
        first, second = gat[c, at, 2 * pair].astype(F32), gat[c, at, 2 * pair + 1].astype(F32)
        return jnp.concatenate([
            jnp.where(lane_c < 64, first, pltpu.roll(second, 64, 1)),
            jnp.where(lane_c < 64, pltpu.roll(first, 64, 1), second),
        ], axis=0)

    squares = []
    for c in range(2):
        parts = [side_by_side(c, across, pair) for pair in range(2)]
        squares.append(jnp.sum(parts[0] * parts[0] + parts[1] * parts[1], axis=1, keepdims=True))
    squares = jnp.concatenate(squares + [jnp.zeros((PADDED - ROWS, 1), F32)], axis=0)
    sq_all[place] = jnp.transpose(jnp.broadcast_to(squares, (PADDED, 128)))[0:1]

    def q_copy(i):
        return copy(sq_all.at[place], sq_all.at[place], q_send.at[i], q_recv.at[place], samp, low * 8 + i)

    for i in range(8):
        @pl.when(place != i)
        def _():
            q_copy(i).start()

    for one in w_copies:
        one.wait_recv()
    e_copies = []
    for c in range(2):
        for one in f_copies[c]:
            one.wait_recv()
        for at in range(4):
            for pair in range(2):
                gathered[:, pl.ds(256 * at + 128 * pair, 128)] = side_by_side(c, at, pair).astype(BF16)
        products = [
            mm(gathered[:, pl.ds(512 * half, 512)], w_all[2 * half:2 * half + 2].reshape(512, 512)) for half in range(2)
        ]
        if c == 0:
            for i in range(8):
                @pl.when(place != i)
                def _():
                    pltpu.make_async_copy(sq_all.at[i], sq_all.at[i], q_recv.at[i]).wait()
            scales = []
            for half in range(2):
                total = sq_all[4 * half] + sq_all[4 * half + 1] + sq_all[4 * half + 2] + sq_all[4 * half + 3]
                scale = jnp.broadcast_to(lax.rsqrt(total * (1.0 / 1024.0) + 1e-5), (128, PADDED))
                scales.append(jnp.transpose(scale))
        scaled = [
            products[half] * jnp.concatenate([scales[half][2 * BLOCK * c:2 * BLOCK * c + 2 * BLOCK]] * 4, axis=1)
            for half in range(2)
        ]
        scaled = scaled[0] + scaled[1]
        product[c, 0] = scaled[:, :256]
        product[c, 1] = scaled[:, 256:]
        e_src[c] = product[c, 1 - core].astype(BF16)
        e_copies += start([
            copy(e_src.at[c], e_dst.at[c], e_send.at[c], e_recv.at[c], samp, low * 8 + across * 2 + 1 - core)
        ])

    def d3_copy(s):
        return copy(d3_src.at[s], d3_dst.at[low], d3_send.at[s], d3_recv.at[low], s, samp * 8 + place)

    def stays(s):
        return jnp.logical_and(samp == low, samp == s)

    for c in range(2):
        e_copies[c].wait_recv()
        outer = jnp.logical_or(samp == 0, samp == 3)
        far = jnp.where(outer, 1 - c, c)
        for half in (far, 1 - far):
            rows = pl.ds(pl.multiple_of(BLOCK * half, 16), BLOCK)
            s = 2 * c + half
            d3_src[s] = (product[c, core, rows, :] + e_dst[c, rows, :].astype(F32)).astype(BF16)

            @pl.when(stays(s))
            def _():
                d3_dst[low] = d3_src[s]

            @pl.when(jnp.logical_not(stays(s)))
            def _():
                d3_copy(s).start()

    for i in range(4):
        @pl.when(jnp.logical_or(low != samp, i != low))
        def _():
            pltpu.make_async_copy(d3_dst.at[i], d3_dst.at[i], d3_recv.at[i]).wait()
    value = d3_dst[0].astype(F32)
    for i in range(1, 4):
        value = value + d3_dst[i].astype(F32)
    rows_ref[...] = value.astype(BF16)

    for i in range(8):
        @pl.when(place != i)
        def _():
            q_copy(i).wait_send()
    for g in range(8):
        @pl.when(g * 4 + low != tp)
        def _():
            a_copy(g).wait_send()
    for one in sends:
        one.wait_send()
    for s in range(4):
        @pl.when(jnp.logical_not(stays(s)))
        def _():
            d3_copy(s).wait_send()


def finish(rows_ref, lengths_ref, prefill_ref, decode_ref):
    prefill_ref[...] = rows_ref[:64]
    step = iota((16, CHANNELS), 0)
    lengths = jnp.zeros((16, CHANNELS), jnp.int32)
    for i in range(4):
        lengths = jnp.where(step % 4 == i, lengths_ref[0, i], lengths)
    decode = jnp.where(step // 4 < lengths, rows_ref[64:].astype(F32), 0.0).astype(BF16)
    for i in range(4):
        decode_ref[i] = decode[4 * i:4 * i + 4]


def shards(
    prompt_tokens, step_tokens, lengths, input_weight, group_weight, step_weight,
    conv_weight, group_conv, conv_bias, group_bias, step_bias, decay_log, skip_gain, norm_gain, output_weight,
):
    anywhere = pl.BlockSpec(memory_space=pl.ANY)
    vector = pl.BlockSpec(memory_space=pltpu.VMEM)

    def dma(*shape):
        return pltpu.SemaphoreType.DMA(shape)

    def room(*shape):
        return pltpu.VMEM(shape, BF16)

    def wide_room(*shape):
        return pltpu.VMEM(shape, F32)

    rows = pl.pallas_call(
        kernel,
        out_shape=jax.ShapeDtypeStruct((BLOCK, CHANNELS), BF16),
        in_specs=[anywhere] * 14,
        out_specs=vector,
        scratch_shapes=[
            room(PADDED, WIDTH), room(2, WIDTH, CHANNELS), room(64, WIDTH), room(CHANNELS, WIDTH), room(4, WIDTH),
            wide_room(4, CHANNELS), wide_room(1, CHANNELS), wide_room(4, 64), wide_room(1, 64),
            wide_room(1, 4), wide_room(1, 4), wide_room(1, 4), wide_room(1, CHANNELS), dma(15),
            wide_room(128, 64),
            room(8, 8, PADDED), room(8, 8, PADDED),
            room(160, 128), room(160, 128), room(2, 160, 128),
            room(4, 64, PADDED),
            room(4, 176, 128), room(176, 128), room(176, 128), room(2, 176, 128),
            room(4, 160, 128), room(160, 128), room(160, 128), room(2, 160, 128),
            room(4, CHANNELS, 512), room(4, CHANNELS, 512),
            room(PADDED, 128), wide_room(576, 128),
            room(2, 4, 4, BLOCK, 128), room(2 * BLOCK, 1024), wide_room(8, 1, PADDED),
            wide_room(2, 2, 2 * BLOCK, CHANNELS), room(2, 2 * BLOCK, CHANNELS), room(2, 2 * BLOCK, CHANNELS),
            room(4, BLOCK, CHANNELS), room(4, BLOCK, CHANNELS),
            dma(8), dma(8), dma(2, 2), dma(2, 2), dma(3), dma(3), dma(6), dma(6), dma(6), dma(6), dma(3), dma(3),
            dma(2, 3), dma(2, 3), dma(2, 4, 3), dma(2, 4, 3), dma(8), dma(8), dma(2), dma(2), dma(4), dma(4),
        ],
        compiler_params=pltpu.CompilerParams(
            collective_id=0, has_side_effects=True, vmem_limit_bytes=VMEM_LIMIT
        ),
        cost_estimate=pl.CostEstimate(flops=2 * 10**9, bytes_accessed=8 * 10**6, transcendentals=10**6),
    )(
        prompt_tokens.reshape(PROMPT, WIDTH),
        step_tokens.reshape(FRESH, WIDTH),
        input_weight,
        group_weight.T,
        output_weight,
        step_weight.T,
        conv_weight,
        conv_bias.reshape(1, CHANNELS),
        group_conv,
        group_bias.reshape(1, 64),
        step_bias.reshape(1, 4),
        decay_log.reshape(1, 4),
        skip_gain.reshape(1, 4),
        norm_gain.reshape(1, CHANNELS),
    )
    prefill, decode = pl.pallas_call(
        finish,
        out_shape=(
            jax.ShapeDtypeStruct((64, CHANNELS), BF16),
            jax.ShapeDtypeStruct((4, 4, CHANNELS), BF16),
        ),
        in_specs=[vector, pl.BlockSpec(memory_space=pltpu.SMEM)],
        out_specs=(vector, vector),
    )(rows, lengths.reshape(1, 4))
    return prefill[:, None, :], decode[:, :, None, :]


def solution(mesh):
    placed = (
        P(None, "rep", "samp"),
        P(None, None, "rep", "samp"),
        P("samp", "rep"),
        P(None, "samp", "tp"),
        P("samp", "tp"),
        P("samp", "tp"),
        P(None, "tp"),
        P(None, "tp"),
        P("tp"),
        P("tp"),
        P("tp"),
        P("tp"),
        P("tp"),
        P("tp"),
        P("tp", "samp"),
    )
    return jax.shard_map(
        shards,
        mesh=mesh,
        in_specs=placed,
        out_specs=(P("samp", "rep", "tp"), P(None, "samp", "rep", "tp")),
        check_vma=False,
    )
```

```python
import jax
import jax.numpy as jnp
from jax import lax
from jax.experimental import pallas as pl
from jax.experimental.pallas import tpu as pltpu
from jax.sharding import PartitionSpec as P

PROMPT = 256
FRESH = 64
ROWS = 320
PADDED = 384
WIDTH = 2048
CHANNELS = 256
BLOCK = 80
VMEM_LIMIT = 60 * 1024 * 1024
MESH = pl.DeviceIdType.MESH
F32 = jnp.float32
BF16 = jnp.bfloat16
NT = (((1,), (1,)), ((), ()))


def mm(a, b):
    return jnp.dot(a, b, preferred_element_type=F32)


def mm_nt(a, b):
    return lax.dot_general(a, b, NT, preferred_element_type=F32)


def iota(shape, axis):
    return lax.broadcasted_iota(jnp.int32, shape, axis)


def silu(v):
    return v / (1.0 + jnp.exp(-v))


def kernel(
    prompt_ref, fresh_ref, in_ref, group_ref, out_ref, step_ref, taps_ref, bias_ref,
    group_taps_ref, group_bias_ref, step_bias_ref, decay_ref, skip_ref, gain_ref,
    rows_ref,
    tokens, w_in, w_group, w_out, w_step, taps_v, bias_v, group_taps_v, group_bias_v,
    step_bias_v, decay_v, skip_v, gain_v, load_sem,
    packed_taps, a_src, a_dst, b_src, b_mid, b_in, maps, x_src, x_by, x_on, x_in, z_src, z_by, z_on, z_in,
    w_src, w_all, mixed, weights, gat, gathered, sq_all,
    product, e_src, e_dst, d3_src, d3_dst,
    a_send, a_recv, b_send, b_recv, c_send, c_recv, x_send, x_recv, z_send, z_recv, w_send, w_recv,
    g_send, g_recv, f_send, f_recv, q_send, q_recv, e_send, e_recv, d3_send, d3_recv,
):
    rep = lax.axis_index("rep")
    samp = lax.axis_index("samp")
    tp = lax.axis_index("tp")
    low = tp // 8
    place = tp % 8
    across = place // 2
    core = place % 2
    group = tp // 4
    quarter = tp % 4

    def device(samp_index, tp_index):
        return (rep, samp_index, tp_index)

    pairs = (
        (group_ref, w_group), (prompt_ref, tokens.at[pl.ds(0, PROMPT)]), (fresh_ref, tokens.at[pl.ds(PROMPT, FRESH)]),
        (group_taps_ref, group_taps_v), (group_bias_ref, group_bias_v), (step_ref, w_step),
        (in_ref.at[1], w_in.at[1]), (in_ref.at[0], w_in.at[0]), (taps_ref, taps_v), (bias_ref, bias_v),
        (step_bias_ref, step_bias_v), (decay_ref, decay_v), (skip_ref, skip_v), (gain_ref, gain_v), (out_ref, w_out),
    )
    loads = [pltpu.make_async_copy(a, b, load_sem.at[i]) for i, (a, b) in enumerate(pairs)]
    for load in loads[:3]:
        load.start()

    barrier = pltpu.get_barrier_semaphore()

    def greet(samp_index, tp_index):
        pl.semaphore_signal(barrier, inc=1, device_id=device(samp_index, tp_index), device_id_type=MESH)

    for d in (2, 1, 3):
        greet((samp + d) % 4, tp)
    for i in range(4):
        @pl.when(jnp.logical_or(low != samp, i != low))
        def _():
            greet(low, i * 8 + place)
    for i in range(8):
        @pl.when(quarter * 8 + i != tp)
        def _():
            greet(samp, quarter * 8 + i)
    for d in range(1, 4):
        greet(samp, group * 4 + (quarter + d) % 4)
        greet(samp, low * 8 + ((across + d) % 4) * 2 + core)
        greet(samp, low * 8 + ((across + d) % 4) * 2 + 1 - core)

    for load in loads[3:]:
        load.start()
    sends = []

    def copy(source, target, send, recv, samp_index, tp_index):
        return pltpu.make_async_remote_copy(
            src_ref=source, dst_ref=target, send_sem=send, recv_sem=recv,
            device_id=device(samp_index, tp_index), device_id_type=MESH,
        )

    def start(copies):
        for one in copies:
            one.start()
            sends.append(one)
        return copies

    tokens[pl.ds(ROWS, PADDED - ROWS), :] = jnp.zeros((PADDED - ROWS, WIDTH), BF16)
    packed_taps[...] = jnp.zeros(packed_taps.shape, F32)
    mixed[pl.ds(ROWS, PADDED - ROWS), :] = jnp.zeros((PADDED - ROWS, 128), BF16)

    row = iota((64, 64), 0)
    col = iota((64, 64), 1)
    regroup = (col == (row % 8) * 8 + row // 8).astype(F32).astype(BF16)
    requarter = (col == ((row % 16) // 4) * 16 + (row // 16) * 4 + row % 4).astype(F32).astype(BF16)

    for load in loads[:5]:
        load.wait()
    for at, value in ((64, group_taps_v[...]), (68, group_bias_v[...])):
        high = value.astype(BF16).astype(F32)
        packed_taps[pl.ds(at, value.shape[0]), :] = high
        packed_taps[pl.ds(at + 8, value.shape[0]), :] = value - high
    maps_partial = mm_nt(w_group[...], tokens[...]).astype(BF16)
    regrouped = mm(regroup, maps_partial)
    tail = regrouped[:, PROMPT:] + mm_nt(regroup, packed_taps[...].astype(BF16))
    a_src[:, :, pl.ds(0, PROMPT)] = regrouped[:, :PROMPT].reshape(8, 8, PROMPT).astype(BF16)
    a_src[:, :, pl.ds(PROMPT, 128)] = tail.reshape(8, 8, 128).astype(BF16)

    pl.semaphore_wait(
        barrier, 22 + jnp.where(quarter != low, 1, 0) + jnp.where(samp != low, 1, 0)
    )

    def a_copy(g):
        return copy(a_src.at[g], a_dst.at[place], a_send.at[g], a_recv.at[place], samp, g * 4 + low)

    for g in range(8):
        @pl.when(g * 4 + low != tp)
        def _():
            a_copy(g).start()

        @pl.when(g * 4 + low == tp)
        def _():
            a_dst[pl.ds(place, 1)] = a_src[pl.ds(g, 1)]

    lane_h = iota((160, 128), 1)

    def packed(part, h):
        upper = part[:160, 128 * (h // 2):128 * (h // 2) + 128]
        lower = part[160:, 128 * (h // 2):128 * (h // 2) + 128]
        if h % 2 == 0:
            return jnp.where(lane_h < 64, upper, pltpu.roll(lower, 64, 1)).astype(BF16)
        return jnp.where(lane_h < 64, pltpu.roll(upper, 64, 1), lower).astype(BF16)

    above, below, opposite = (samp + 1) % 4, (samp + 3) % 4, (samp + 2) % 4

    def first_leg(source, by, into, send, recv, part=slice(4)):
        top, rest = pl.ds(0, BLOCK), pl.ds(BLOCK, source.shape[1] - BLOCK)
        return start([
            copy(source.at[opposite, top], by.at[top], send.at[0], recv.at[0], above, tp),
            copy(source.at[opposite, rest], by.at[rest], send.at[1], recv.at[1], below, tp),
            copy(source.at[above, rest], into.at[0, rest], send.at[2], recv.at[2], above, tp),
            copy(source.at[below, top], into.at[1, top], send.at[3], recv.at[3], below, tp),
        ][part])

    def second_leg(first, source, by, on, into, send, recv):
        top, rest = pl.ds(0, BLOCK), pl.ds(BLOCK, source.shape[1] - BLOCK)
        copies = []
        for i, (rows, to) in enumerate(((top, above), (rest, below))):
            first[i].wait_recv()
            on[rows, :] = (source[to, rows, :].astype(F32) + by[rows, :].astype(F32)).astype(BF16)
            copies += start([copy(on.at[rows], into.at[i, rows], send.at[4 + i], recv.at[4 + i], to, tp)])
        return first[2:] + copies

    loads[5].wait()
    sizes = mm_nt(w_step[...], tokens[...])
    loads[6].wait()
    head_part = mm(tokens[pl.ds(0, ROWS), :], w_in[1])
    size_row = iota((16, 128), 0)
    for h in range(4):
        x_src[h, pl.ds(0, 160), :] = packed(head_part, h)
        piece = jnp.zeros((16, 128), F32)
        for b in range(3):
            piece = jnp.where(size_row == b, sizes[h:h + 1, 128 * b:128 * b + 128], piece)
        x_src[h, pl.ds(160, 16), :] = piece.astype(BF16)
    x_copies = first_leg(x_src, x_by, x_in, x_send, x_recv)
    for load in loads[13:]:
        load.wait()
    gain = jnp.transpose(jnp.broadcast_to(gain_v[...], (128, CHANNELS)))
    for to in range(4):
        for part in range(4):
            columns = pl.ds(512 * to + 128 * part, 128)
            w_src[to, :, pl.ds(128 * part, 128)] = (w_out[:, columns].astype(F32) * gain).astype(BF16)
    w_all[pl.ds(across, 1)] = w_src[pl.ds(across, 1)]
    w_copies = start([
        copy(
            w_src.at[(across + d) % 4], w_all.at[across], w_send.at[d - 1], w_recv.at[d - 1],
            samp, low * 8 + ((across + d) % 4) * 2 + core,
        )
        for d in (2, 1, 3)
    ])

    loads[7].wait()
    gate_part = mm(tokens[pl.ds(0, ROWS), :], w_in[0])
    for h in range(4):
        z_src[h] = packed(gate_part, h)

    z_copies = first_leg(z_src, z_by, z_in, z_send, z_recv, slice(2))

    for i in range(8):
        @pl.when(quarter * 8 + i != tp)
        def _():
            pltpu.make_async_copy(a_dst.at[i], a_dst.at[i], a_recv.at[i]).wait()
    own_maps = a_dst[...].astype(F32).reshape(64, PADDED)
    lane_q = iota((32, 128), 1)
    fresh_maps = own_maps[:, PROMPT:]
    b_src[pl.ds(0, 64), :] = own_maps[:, 0:128].astype(BF16)
    b_src[pl.ds(64, 64), :] = own_maps[:, 128:256].astype(BF16)
    b_src[pl.ds(128, 32), :] = jnp.where(lane_q < 64, fresh_maps[:32], pltpu.roll(fresh_maps[32:], 64, 1)).astype(BF16)
    pairings = (samp + 1 - 2 * (samp % 2), 3 - samp)
    b_rows = (pl.ds(0, BLOCK), pl.ds(BLOCK, BLOCK))

    def b_step(step, source):
        copies = []
        for i, rows in enumerate(b_rows):
            if step == 1:
                b_copies[i].wait_recv()
                b_mid[rows, :] = (b_src[rows, :].astype(F32) + b_in[0, rows, :].astype(F32)).astype(BF16)
            copies += start([
                copy(
                    source.at[rows], b_in.at[step, rows], b_send.at[step, i], b_recv.at[step, i],
                    pairings[(i + step) % 2], tp,
                )
            ])
        return copies

    b_copies = b_step(0, b_src)

    x_copies = second_leg(x_copies, x_src, x_by, x_on, x_in, x_send, x_recv)
    b_copies = b_step(1, b_mid)

    lane128 = iota((1, 128), 1)

    def of_head(value):
        chosen = jnp.zeros((value.shape[0], 128), F32)
        for h in range(4):
            half = value[:, 128 * (h // 2):128 * (h // 2) + 128]
            if h % 2 == 0:
                half = pltpu.roll(half, 64, 1)
            chosen = jnp.where(samp == h, half, chosen)
        return jnp.where(lane128 >= 64, chosen, 0.0)

    def own_scalar(ref):
        return jnp.sum(jnp.where(iota((1, 4), 1) == samp, ref[...], 0.0), axis=1, keepdims=True)

    def unpacked(value):
        return jnp.concatenate([pltpu.roll(value, 64, 1), value], axis=0)

    for load in loads[8:13]:
        load.wait()
    taps8 = of_head(jnp.concatenate([taps_v[...], bias_v[...], jnp.zeros((3, CHANNELS), F32)], axis=0))
    skip = own_scalar(skip_v)
    step_bias = own_scalar(step_bias_v)
    rate = jnp.exp(own_scalar(decay_v))
    z_copies += first_leg(z_src, z_by, z_in, z_send, z_recv, slice(2, 4))
    z_copies = second_leg(z_copies, z_src, z_by, z_on, z_in, z_send, z_recv)
    for one in x_copies:
        one.wait_recv()
    summed = x_src[samp].astype(F32) + x_in[0].astype(F32) + x_in[1].astype(F32)
    summed = summed.astype(BF16).astype(F32)
    heads = unpacked(summed[:160])
    before = heads[:PROMPT]
    row_p = iota((PROMPT, 128), 0)
    conv = taps8[4:5] + taps8[3:4] * before
    for k in range(1, 4):
        conv = conv + taps8[3 - k:4 - k] * jnp.where(row_p >= k, pltpu.roll(before, k, 0), 0.0)
    mixed[pl.ds(0, PROMPT), :] = silu(conv).astype(BF16)
    line = jnp.concatenate(
        [jnp.broadcast_to(before[253 + k:254 + k], (16, 128)) for k in range(3)] + [heads[PROMPT:ROWS]], axis=0
    )
    conv = taps8[4:5] + taps8[0:1] * line[0:64]
    for k in range(1, 4):
        conv = conv + taps8[k:k + 1] * line[16 * k:16 * k + 64]
    mixed[pl.ds(PROMPT, FRESH), :] = silu(conv).astype(BF16)

    size = jnp.concatenate([summed[160 + b:161 + b] for b in range(3)], axis=1)
    size = jnp.broadcast_to(size, (8, PADDED)) + step_bias
    size = jnp.maximum(size, 0.0) + jnp.log1p(jnp.exp(-jnp.abs(size)))
    logs = -size * rate
    run = logs[:, :PROMPT]
    lane_r = iota((8, PROMPT), 1)
    for k in (1, 2, 4, 8, 16, 32, 64, 128):
        run = run + jnp.where(lane_r >= k, pltpu.roll(run, k, 1), 0.0)
    run_f = logs[:, PROMPT:]
    lane_s = iota((8, 128), 1)
    for k in (16, 32):
        run_f = run_f + jnp.where(lane_s >= k, pltpu.roll(run_f, k, 1), 0.0)
    run_f = run_f + run[:, PROMPT - 1:PROMPT]
    runs = [run[0:1, 0:128], run[0:1, 128:256], run_f[0:1]]
    trail = jnp.concatenate([jnp.transpose(jnp.broadcast_to(r, (128, 128))) for r in runs], axis=0)[:ROWS]
    lane = iota((128, 128), 1)
    row_q = iota((128, 128), 0)
    tiles = ((256, 64, 0), (256, 64, 1), (256, 64, 2), (0, 128, 0), (128, 128, 0), (128, 128, 1))
    offsets = (0, 64, 128, 192, 320, 448)
    for (first, count, b), offset in zip(tiles, offsets):
        gap = trail[first:first + count] - runs[b]
        if b == 2:
            seen = jnp.logical_and(lane <= row_q, lane % 16 == row_q % 16)[:count]
            gap = jnp.where(seen, gap, -1e30)
        elif first == 128 * b:
            gap = jnp.where(lane <= row_q, gap, -1e30)
        weights[pl.ds(offset, count), :] = jnp.exp(gap) * size[0:1, 128 * b:128 * b + 128]

    for one in b_copies:
        one.wait_recv()
    total = b_mid[...].astype(F32) + b_in[1].astype(F32)
    total = total.astype(BF16).astype(F32)
    taps = [own_maps[:, 320 + k:321 + k] + own_maps[:, 328 + k:329 + k] for k in range(5)]
    before = jnp.concatenate([total[0:64], total[64:128]], axis=1)
    lane_p = iota((64, PROMPT), 1)
    conv = taps[4] + taps[3] * before
    for k in range(1, 4):
        conv = conv + taps[3 - k] * jnp.where(lane_p >= k, pltpu.roll(before, k, 1), 0.0)
    maps_prompt = silu(conv).astype(BF16)
    lane_f = iota((64, 128), 1)
    line = jnp.concatenate([total[128:160], pltpu.roll(total[128:160], 64, 1)], axis=0)
    line = pltpu.roll(line, 48, 1)
    for k in range(3):
        line = jnp.where(
            jnp.logical_and(lane_f >= 16 * k, lane_f < 16 * k + 16), before[:, 253 + k:254 + k], line
        )
    conv = taps[4] + taps[0] * line
    for k in range(1, 4):
        conv = conv + taps[k] * pltpu.roll(line, 128 - 16 * k, 1)
    maps_fresh = jnp.where(lane_f < 64, silu(conv), 0.0).astype(BF16)
    maps[quarter, :, pl.ds(0, PROMPT)] = maps_prompt
    maps[quarter, :, pl.ds(PROMPT, 128)] = maps_fresh
    c_copies = start([
        copy(maps.at[quarter], maps.at[quarter], c_send.at[d - 1], c_recv.at[d - 1], samp, group * 4 + (quarter + d) % 4)
        for d in (3, 2, 1)
    ])
    for one in c_copies:
        one.wait_recv()
    inputs = jnp.concatenate([maps[0], maps[1]], axis=0)
    to_read = jnp.concatenate([maps[2], maps[3]], axis=0).astype(F32)
    readout = jnp.transpose(to_read).astype(BF16)

    def read(first, count, blocks):
        value = skip * mixed[pl.ds(first, count), :].astype(F32)
        for b, offset in blocks:
            products = mm(readout[first:first + count], inputs[:, 128 * b:128 * b + 128])
            seen = (weights[pl.ds(offset, count), :] * products).astype(BF16)
            value = value + mm(seen, mixed[pl.ds(128 * b, 128), :])
        return value

    fresh = read(256, 64, ((0, 0), (1, 64), (2, 128)))
    halves = [read(0, 128, ((0, 192),)), read(128, 128, ((0, 320), (1, 448)))]
    for one in z_copies:
        one.wait_recv()
    gate = z_src[samp].astype(F32) + z_in[0].astype(F32) + z_in[1].astype(F32)
    gate = silu(unpacked(gate.astype(BF16).astype(F32)))
    fresh = mm(requarter, (fresh * gate[PROMPT:]).astype(BF16))

    lane_c = iota((BLOCK, 128), 1)

    def onward(c, k):
        piece = (samp - k + 4) % 4
        return start([
            copy(
                gat.at[c, across, piece], gat.at[c, across, piece], f_send.at[c, k, d - 1], f_recv.at[c, k, d - 1],
                samp, low * 8 + ((across + d) % 4) * 2 + core,
            )
            for d in (2, 1, 3)
        ])

    for c in range(2):
        gated = halves[c] * gate[128 * c:128 * c + 128]
        upper = jnp.concatenate([gated[:64], fresh[32 * c:32 * c + 16]], axis=0)
        lower = jnp.concatenate([gated[64:], fresh[32 * c + 16:32 * c + 32]], axis=0)
        gat[c, across, samp] = jnp.where(lane_c < 64, pltpu.roll(upper, 64, 1), lower).astype(BF16)
    g_copies = [{}, {}]
    for d in (2, 1, 3):
        for c in range(2):
            g_copies[c][d] = start([
                copy(
                    gat.at[c, across, samp], gat.at[c, across, samp], g_send.at[c, d - 1], g_recv.at[c, d - 1],
                    (samp + d) % 4, tp,
                )
            ])[0]
    f_copies = [onward(c, 0) for c in range(2)]
    for k in (1, 3, 2):
        for c in range(2):
            g_copies[c][k].wait_recv()
            f_copies[c] += onward(c, k)

    def side_by_side(c, at, pair):
        first, second = gat[c, at, 2 * pair].astype(F32), gat[c, at, 2 * pair + 1].astype(F32)
        return jnp.concatenate([
            jnp.where(lane_c < 64, first, pltpu.roll(second, 64, 1)),
            jnp.where(lane_c < 64, pltpu.roll(first, 64, 1), second),
        ], axis=0)

    squares = []
    for c in range(2):
        parts = [side_by_side(c, across, pair) for pair in range(2)]
        squares.append(jnp.sum(parts[0] * parts[0] + parts[1] * parts[1], axis=1, keepdims=True))
    squares = jnp.concatenate(squares + [jnp.zeros((PADDED - ROWS, 1), F32)], axis=0)
    sq_all[place] = jnp.transpose(jnp.broadcast_to(squares, (PADDED, 128)))[0:1]

    def q_copy(i):
        return copy(sq_all.at[place], sq_all.at[place], q_send.at[i], q_recv.at[place], samp, low * 8 + i)

    for i in range(8):
        @pl.when(place != i)
        def _():
            q_copy(i).start()

    for one in w_copies:
        one.wait_recv()
    e_copies = []
    for c in range(2):
        for one in f_copies[c]:
            one.wait_recv()
        for at in range(4):
            for pair in range(2):
                gathered[:, pl.ds(256 * at + 128 * pair, 128)] = side_by_side(c, at, pair).astype(BF16)
        products = [
            mm(gathered[:, pl.ds(512 * half, 512)], w_all[2 * half:2 * half + 2].reshape(512, 512)) for half in range(2)
        ]
        if c == 0:
            for i in range(8):
                @pl.when(place != i)
                def _():
                    pltpu.make_async_copy(sq_all.at[i], sq_all.at[i], q_recv.at[i]).wait()
            scales = []
            for half in range(2):
                total = sq_all[4 * half] + sq_all[4 * half + 1] + sq_all[4 * half + 2] + sq_all[4 * half + 3]
                scale = jnp.broadcast_to(lax.rsqrt(total * (1.0 / 1024.0) + 1e-5), (128, PADDED))
                scales.append(jnp.transpose(scale))
        scaled = [
            products[half] * jnp.concatenate([scales[half][2 * BLOCK * c:2 * BLOCK * c + 2 * BLOCK]] * 4, axis=1)
            for half in range(2)
        ]
        scaled = scaled[0] + scaled[1]
        product[c, 0] = scaled[:, :256]
        product[c, 1] = scaled[:, 256:]
        e_src[c] = product[c, 1 - core].astype(BF16)
        e_copies += start([
            copy(e_src.at[c], e_dst.at[c], e_send.at[c], e_recv.at[c], samp, low * 8 + across * 2 + 1 - core)
        ])

    def d3_copy(s):
        return copy(d3_src.at[s], d3_dst.at[low], d3_send.at[s], d3_recv.at[low], s, samp * 8 + place)

    def stays(s):
        return jnp.logical_and(samp == low, samp == s)

    for c in range(2):
        e_copies[c].wait_recv()
        outer = jnp.logical_or(samp == 0, samp == 3)
        far = jnp.where(outer, 1 - c, c)
        for half in (far, 1 - far):
            rows = pl.ds(pl.multiple_of(BLOCK * half, 16), BLOCK)
            s = 2 * c + half
            d3_src[s] = (product[c, core, rows, :] + e_dst[c, rows, :].astype(F32)).astype(BF16)

            @pl.when(stays(s))
            def _():
                d3_dst[low] = d3_src[s]

            @pl.when(jnp.logical_not(stays(s)))
            def _():
                d3_copy(s).start()

    for i in range(4):
        @pl.when(jnp.logical_or(low != samp, i != low))
        def _():
            pltpu.make_async_copy(d3_dst.at[i], d3_dst.at[i], d3_recv.at[i]).wait()
    value = d3_dst[0].astype(F32)
    for i in range(1, 4):
        value = value + d3_dst[i].astype(F32)
    rows_ref[...] = value.astype(BF16)

    for i in range(8):
        @pl.when(place != i)
        def _():
            q_copy(i).wait_send()
    for g in range(8):
        @pl.when(g * 4 + low != tp)
        def _():
            a_copy(g).wait_send()
    for one in sends:
        one.wait_send()
    for s in range(4):
        @pl.when(jnp.logical_not(stays(s)))
        def _():
            d3_copy(s).wait_send()


def finish(rows_ref, lengths_ref, prefill_ref, decode_ref):
    prefill_ref[...] = rows_ref[:64]
    step = iota((16, CHANNELS), 0)
    lengths = jnp.zeros((16, CHANNELS), jnp.int32)
    for i in range(4):
        lengths = jnp.where(step % 4 == i, lengths_ref[0, i], lengths)
    decode = jnp.where(step // 4 < lengths, rows_ref[64:].astype(F32), 0.0).astype(BF16)
    for i in range(4):
        decode_ref[i] = decode[4 * i:4 * i + 4]


def shards(
    prompt_tokens, step_tokens, lengths, input_weight, group_weight, step_weight,
    conv_weight, group_conv, conv_bias, group_bias, step_bias, decay_log, skip_gain, norm_gain, output_weight,
):
    anywhere = pl.BlockSpec(memory_space=pl.ANY)
    vector = pl.BlockSpec(memory_space=pltpu.VMEM)

    def dma(*shape):
        return pltpu.SemaphoreType.DMA(shape)

    def room(*shape):
        return pltpu.VMEM(shape, BF16)

    def wide_room(*shape):
        return pltpu.VMEM(shape, F32)

    rows = pl.pallas_call(
        kernel,
        out_shape=jax.ShapeDtypeStruct((BLOCK, CHANNELS), BF16),
        in_specs=[anywhere] * 14,
        out_specs=vector,
        scratch_shapes=[
            room(PADDED, WIDTH), room(2, WIDTH, CHANNELS), room(64, WIDTH), room(CHANNELS, WIDTH), room(4, WIDTH),
            wide_room(4, CHANNELS), wide_room(1, CHANNELS), wide_room(4, 64), wide_room(1, 64),
            wide_room(1, 4), wide_room(1, 4), wide_room(1, 4), wide_room(1, CHANNELS), dma(15),
            wide_room(128, 64),
            room(8, 8, PADDED), room(8, 8, PADDED),
            room(160, 128), room(160, 128), room(2, 160, 128),
            room(4, 64, PADDED),
            room(4, 176, 128), room(176, 128), room(176, 128), room(2, 176, 128),
            room(4, 160, 128), room(160, 128), room(160, 128), room(2, 160, 128),
            room(4, CHANNELS, 512), room(4, CHANNELS, 512),
            room(PADDED, 128), wide_room(576, 128),
            room(2, 4, 4, BLOCK, 128), room(2 * BLOCK, 1024), wide_room(8, 1, PADDED),
            wide_room(2, 2, 2 * BLOCK, CHANNELS), room(2, 2 * BLOCK, CHANNELS), room(2, 2 * BLOCK, CHANNELS),
            room(4, BLOCK, CHANNELS), room(4, BLOCK, CHANNELS),
            dma(8), dma(8), dma(2, 2), dma(2, 2), dma(3), dma(3), dma(6), dma(6), dma(6), dma(6), dma(3), dma(3),
            dma(2, 3), dma(2, 3), dma(2, 4, 3), dma(2, 4, 3), dma(8), dma(8), dma(2), dma(2), dma(4), dma(4),
        ],
        compiler_params=pltpu.CompilerParams(
            collective_id=0, has_side_effects=True, vmem_limit_bytes=VMEM_LIMIT
        ),
        cost_estimate=pl.CostEstimate(flops=2 * 10**9, bytes_accessed=8 * 10**6, transcendentals=10**6),
    )(
        prompt_tokens.reshape(PROMPT, WIDTH),
        step_tokens.reshape(FRESH, WIDTH),
        input_weight,
        group_weight.T,
        output_weight,
        step_weight.T,
        conv_weight,
        conv_bias.reshape(1, CHANNELS),
        group_conv,
        group_bias.reshape(1, 64),
        step_bias.reshape(1, 4),
        decay_log.reshape(1, 4),
        skip_gain.reshape(1, 4),
        norm_gain.reshape(1, CHANNELS),
    )
    prefill, decode = pl.pallas_call(
        finish,
        out_shape=(
            jax.ShapeDtypeStruct((64, CHANNELS), BF16),
            jax.ShapeDtypeStruct((4, 4, CHANNELS), BF16),
        ),
        in_specs=[vector, pl.BlockSpec(memory_space=pltpu.SMEM)],
        out_specs=(vector, vector),
    )(rows, lengths.reshape(1, 4))
    return prefill[:, None, :], decode[:, :, None, :]


def solution(mesh):
    placed = (
        P(None, "rep", "samp"),
        P(None, None, "rep", "samp"),
        P("samp", "rep"),
        P(None, "samp", "tp"),
        P("samp", "tp"),
        P("samp", "tp"),
        P(None, "tp"),
        P(None, "tp"),
        P("tp"),
        P("tp"),
        P("tp"),
        P("tp"),
        P("tp"),
        P("tp"),
        P("tp", "samp"),
    )
    return jax.shard_map(
        shards,
        mesh=mesh,
        in_specs=placed,
        out_specs=(P("samp", "rep", "tp"), P(None, "samp", "rep", "tp")),
        check_vma=False,
    )
```
